32 devices in a mesh: seq: 8 (over z, y), ch: 4 (over x, core).
Axes of the slice: x: 2, y: 2, z: 4, core: 2. Of those that a mesh axis runs over, the one named last changes fastest.
Arguments:
- value_in: bfloat16 [4096, 1024], P('ch', 'seq'), may hold values from -6 to 6
- gate_inner: bfloat16 [4096, 1024], P('ch', 'seq'), may hold values from -6 to 6
- gate_outer: bfloat16 [4096, 1024], P('ch', 'seq'), may hold values from -6 to 6
- out_grad: bfloat16 [4096, 1024], P('ch', 'seq'), may hold values from -6 to 6
- filter_proj: bfloat16 [2, 4096, 64], P(None, 'ch'), may hold values from -0.75 to 0.75
- decay: float32 [2, 4096], P(None, 'ch'), may hold values from 0.00048828125 to 0.05
- frequency: float32 [64], replicated, may hold values from 0.001 to 3
Outputs:
- grad_value: bfloat16 [4096, 1024], P('ch', 'seq')
- grad_gate_inner: bfloat16 [4096, 1024], P('ch', 'seq')
- grad_gate_outer: bfloat16 [4096, 1024], P('ch', 'seq')
- filter_grad: float32 [2, 4096, 64], P(None, 'ch')
The draws below stay inside these ranges and needn't reach their ends.
All inputs are finite; a program needn't handle non-finite values.
Results may differ from the reference program's by a relative error of at most 0.0025.
Values may be sent and summed in bfloat16 or wider, within the bound.
No kernel may reach another device: no remote copies, remote signals or barrier semaphores. Data moves between devices by JAX's collectives and lax.ppermute only.
A program may use at most 64 MiB of HBM per device.

```python
import math
import jax
import jax.numpy as jnp
from jax import lax

D = 4096
F = 64
SEQ = 1024


def shard_levels(stream_key, extent, shards, least, top_value):
    def one(axis_at, blocks):
        steps = jax.random.uniform(jax.random.fold_in(jax.random.fold_in(stream_key, 6), axis_at), (blocks,), jnp.float32, least / len(shards), top_value / len(shards))
        return jnp.repeat(jnp.exp(steps), extent[axis_at] // blocks).reshape((-1,) + (1,) * (len(extent) - axis_at - 1))

    factor_of = one(*shards[0])
    for cut in shards[1:]:
        factor_of = factor_of * one(*cut)
    return factor_of


def noise(key, extent, width, bound, cuts=(), held_as=jnp.bfloat16):
    level = shard_levels(key, extent, cuts, -0.22, 0.18) if cuts else 1.0
    array = jax.random.normal(key, extent, jnp.float32) * width * level
    return jnp.minimum(jnp.maximum(array, -bound), bound).astype(held_as)


def setup_inputs(seed: int = 0) -> dict:
    seeds = jax.random.split(jax.random.key(seed), 8)
    return {
        "value_in": noise(seeds[0], (D, SEQ), 1.0, 6.0, ((0, 4), (1, 8))),
        "gate_inner": noise(seeds[1], (D, SEQ), 1.0, 6.0, ((0, 4), (1, 8))),
        "gate_outer": noise(seeds[2], (D, SEQ), 1.0, 6.0, ((0, 4), (1, 8))),
        "out_grad": noise(seeds[3], (D, SEQ), 1.0, 6.0, ((0, 4), (1, 8))),
        "filter_proj": noise(seeds[4], (2, D, F), F ** -0.5, 0.75, ((1, 4),)),
        "decay": jnp.clip(jnp.exp(math.log(0.05) - 4.6288867 * jax.random.uniform(seeds[5], (2, D), jnp.float32) ** shard_levels(seeds[5], (2, D), ((1, 4),), -0.2, 0.2)), 0.00048828125, 0.05),
        "frequency": jnp.clip(jnp.exp(jax.random.uniform(seeds[6], (F,), jnp.float32, math.log(0.001), math.log(3.0))), 0.001, 3.0),
    }


def reference(value_in, gate_inner, gate_outer, out_grad, filter_proj, decay, frequency):
    length = SEQ
    highest = lax.Precision.HIGHEST
    positions = jnp.arange(length, dtype=jnp.float32)
    features = jnp.sin(frequency[None, :] * (positions[:, None] + 1.0))
    rows = math.gcd(D, 256)
    blocks = D // rows

    def spectrum(signal):
        return jnp.fft.rfft(signal, n=2 * length, axis=-1)

    def restore(spec):
        return jnp.fft.irfft(spec, n=2 * length, axis=-1)[..., :length].astype(jnp.float32)

    def one_block(items):
        value_blk, inner_blk, outer_blk, grad_blk, proj_blk, rates = items
        value_f = value_blk.astype(jnp.float32)
        inner_f = inner_blk.astype(jnp.float32)
        outer_f = outer_blk.astype(jnp.float32)
        grad_f = grad_blk.astype(jnp.float32)
        window = jnp.sqrt(2.0 * rates)[:, :, None] * jnp.exp(-rates[:, :, None] * positions)
        filters = jnp.einsum('kdf,tf->kdt', proj_blk.astype(jnp.float32), features, precision=highest) * window
        inner_spec = spectrum(filters[0])
        outer_spec = spectrum(filters[1])
        value_spec = spectrum(value_f)
        inner_act = restore(inner_spec * value_spec)
        mixed = inner_f * inner_act
        mixed_spec = spectrum(mixed)
        outer_act = restore(outer_spec * mixed_spec)
        grad_outer = grad_f * outer_act
        grad_spec = spectrum(grad_f * outer_f)
        grad_mixed = restore(jnp.conj(outer_spec) * grad_spec)
        grad_outer_filter = restore(jnp.conj(mixed_spec) * grad_spec)
        grad_inner = grad_mixed * inner_act
        inner_grad_spec = spectrum(grad_mixed * inner_f)
        grad_value = restore(jnp.conj(inner_spec) * inner_grad_spec)
        grad_inner_filter = restore(jnp.conj(value_spec) * inner_grad_spec)
        weighted = jnp.stack([grad_inner_filter, grad_outer_filter]) * window
        proj_grad = jnp.einsum('kdt,tf->kdf', weighted, features, precision=highest)
        return (grad_value.astype(jnp.bfloat16), grad_inner.astype(jnp.bfloat16), grad_outer.astype(jnp.bfloat16), proj_grad)
    items = (value_in.reshape(blocks, rows, length), gate_inner.reshape(blocks, rows, length), gate_outer.reshape(blocks, rows, length), out_grad.reshape(blocks, rows, length), filter_proj.reshape(2, blocks, rows, F).transpose(1, 0, 2, 3), decay.reshape(2, blocks, rows).transpose(1, 0, 2))
    grad_value, grad_inner, grad_outer, proj_grad = lax.map(one_block, items)
    proj_grad = proj_grad.transpose(1, 0, 2, 3).reshape(2, D, F)
    scale = lax.rsqrt(jnp.mean(proj_grad * proj_grad) + 1e-06)
    return (grad_value.reshape(D, length), grad_inner.reshape(D, length), grad_outer.reshape(D, length), proj_grad * scale)
```

```python
import math
import functools
import numpy as np
import ml_dtypes
import jax
import jax.numpy as jnp
from jax import lax
from jax.experimental import pallas as pl
from jax.experimental.pallas import tpu as pltpu
from jax.sharding import PartitionSpec as P

BLOCKS = 8
LANES = 128
COS1, COS2, COS3 = (math.cos(math.pi / 8), math.cos(math.pi / 4), math.cos(3 * math.pi / 8))
STEP = 16


def class_tables():
    points = BLOCKS * LANES * 2
    lane = np.arange(LANES)
    forward = np.zeros((BLOCKS, 2 * LANES, 2 * LANES))
    inverse = np.zeros((BLOCKS, 2 * LANES, 2 * LANES))
    for residue in range(1, BLOCKS):
        angle = 2 * np.pi * np.outer(lane, 16 * lane + residue) / points
        cos, sin = np.cos(angle), np.sin(angle)
        forward[residue] = np.block([[cos, -sin], [-sin, -cos]])
        inverse[residue] = np.block([[cos.T, sin.T], [-sin.T, cos.T]]) * (2.0 / points)
    half = LANES // 2
    for offset, first in ((0, 0), (8, half)):
        angle = 2 * np.pi * np.outer(lane, 16 * lane[:half] + offset) / points
        cos, sin = np.cos(angle), np.sin(angle)
        rows = slice(0, LANES) if offset == 0 else slice(LANES, 2 * LANES)
        re_cols, im_cols = slice(first, first + half), slice(LANES + first, LANES + first + half)
        forward[0, rows, re_cols] = cos
        forward[0, rows, im_cols] = -sin
        inverse[0, re_cols, rows] = cos.T * (2.0 / points)
        inverse[0, im_cols, rows] = -sin.T * (2.0 / points)
    forward[0, :LANES, LANES] = (-1.0) ** lane
    inverse[0, 0, :LANES] = 1.0 / points
    inverse[0, LANES, :LANES] = (-1.0) ** lane / points
    return forward, inverse


def split_table(table):
    high = table.astype(ml_dtypes.bfloat16)
    low = (table - high.astype(np.float64)).astype(ml_dtypes.bfloat16)
    return high, low


def fold(x):
    s = [x[a] + x[a + 4] for a in range(4)]
    d = [x[a] - x[a + 4] for a in range(4)]
    t0, t1 = s[0] + s[2], s[1] + s[3]
    u0, u1 = s[0] - s[2], s[1] - s[3]
    p, w = (d[1] - d[3]) * COS2, (d[1] + d[3]) * COS2
    p1, p2, p3 = x[1] - x[7], (x[2] - x[6]) * COS2, x[3] - x[5]
    n1, n2, n3 = x[1] + x[7], (x[2] + x[6]) * COS2, x[3] + x[5]
    a0, b0 = x[0] + p2, x[0] - p2
    c0, d0 = p1 * COS1 + p3 * COS3, p1 * COS3 - p3 * COS1
    a1, b1 = n2 + x[4], n2 - x[4]
    c1, d1 = n1 * COS3 + n3 * COS1, n1 * COS1 - n3 * COS3
    return (
        (t0 + t1, t0 - t1),
        (a0 + c0, c1 + a1),
        (d[0] + p, d[2] + w),
        (b0 + d0, d1 + b1),
        (u0, u1),
        (b0 - d0, d1 - b1),
        (d[0] - p, w - d[2]),
        (a0 - c0, c1 - a1),
    )


def unfold(z):
    (z0, z8), (r1, i1), (r2, i2), (r3, i3), (r4, i4), (r5, i5), (r6, i6), (r7, i7) = z
    even, odd = z0 + z8, z0 - z8
    g = [even + r4, odd - i4, even - r4, odd + i4]
    dr, di = r2 - r6, i2 + i6
    h = [r2 + r6, (dr - di) * COS2, i6 - i2, (dr + di) * -COS2]
    rs, rd, ts, td = r1 + r7, r1 - r7, r3 + r5, r3 - r5
    js, jd, ks, kd = i1 + i7, i1 - i7, i3 + i5, i3 - i5
    k = [None, rd * COS1 + td * COS3, (rs - ts) * COS2, rd * COS3 - td * COS1]
    m = [None, js * COS3 + ks * COS1, (jd + kd) * COS2, js * COS1 - ks * COS3]
    o = [rs + ts, k[1] - m[1], k[2] - m[2], k[3] - m[3], kd - jd, -(k[3] + m[3]), -(k[2] + m[2]), -(k[1] + m[1])]
    return [g[a] + h[a] + o[a] for a in range(4)] + [g[a] - h[a] + o[a + 4] for a in range(4)]


def halves(x):
    high = x.astype(jnp.bfloat16)
    return high, (x - high.astype(jnp.float32)).astype(jnp.bfloat16)


def split_features(features):
    high = lax.reduce_precision(features, 8, 7)
    return high.astype(jnp.bfloat16), (features - high).astype(jnp.bfloat16)


def put(hi_ref, lo_ref, index, parts):
    for part, x in enumerate(parts):
        high, low = halves(x)
        lanes = slice(part * LANES, (part + 1) * LANES)
        hi_ref[index + (lanes,)] = high
        lo_ref[index + (lanes,)] = low


def store_folded(hi_ref, lo_ref, rows, blocks):
    for residue, parts in enumerate(fold(blocks)):
        put(hi_ref, lo_ref, (residue, rows), parts)


def times(high, low, table_hi, table_lo):
    dot = functools.partial(jnp.dot, preferred_element_type=jnp.float32)
    return dot(high, table_hi) + (dot(low, table_hi) + dot(high, table_lo))


def multiplied(left, right, conj, residue):
    a_re, a_im = left
    b_re, b_im = right
    rr, ii, ri, ir = a_re * b_re, a_im * b_im, a_re * b_im, a_im * b_re
    if conj:
        re, im = rr + ii, ri - ir
    else:
        re, im = rr - ii, ri + ir
    if residue == 0:
        shared = lax.broadcasted_iota(jnp.int32, re.shape, 1) == 0
        re, im = jnp.where(shared, rr, re), jnp.where(shared, ii, im)
    return re, im


def window_blocks(rate):
    rate = jnp.broadcast_to(rate, (rate.shape[0], LANES))
    place = lax.broadcasted_iota(jnp.int32, rate.shape, 1).astype(jnp.float32)
    first = jnp.sqrt(2.0 * rate) * jnp.exp(-rate * place)
    return [first * jnp.exp(rate * (-float(LANES) * a)) if a else first for a in range(BLOCKS)]


def filter_kernel(proj, rate, features, table_hi, table_lo, spectra, filters, fold_hi, fold_lo):
    rows = proj.shape[0]
    for a in range(BLOCKS):
        filters[a] = jnp.dot(proj[...], features[a], preferred_element_type=jnp.float32)

    @pl.loop(0, rows // STEP)
    def _(step):
        at = pl.ds(pl.multiple_of(step * STEP, STEP), STEP)
        window = window_blocks(rate[at, :])
        store_folded(fold_hi, fold_lo, at, [filters[a, at, :] * window[a] for a in range(BLOCKS)])

    for residue in range(BLOCKS):
        spectra[residue] = times(fold_hi[residue], fold_lo[residue], table_hi[residue], table_lo[residue])


def main_kernel(
    moved, rate, filt, feat_hi, feat_lo, fwd_hi, fwd_lo, inv_hi, inv_lo,
    grads, proj_grad,
    one_hi, one_lo, two_hi, two_lo, spec, spec2, back, weighted_hi, weighted_lo,
):
    count = moved.shape[1] // 4
    value, inner, outer, grad = (moved.at[:, i * count : (i + 1) * count] for i in range(4))
    grad_value, grad_inner, grad_outer = (grads.at[:, i * count : (i + 1) * count] for i in range(3))

    def chunk(step):
        return pl.ds(pl.multiple_of(step * STEP, STEP), STEP), pl.ds(pl.multiple_of(count + step * STEP, STEP), STEP)

    def pair(ref, residue, rows):
        return ref[residue, rows, :LANES], ref[residue, rows, LANES:]

    upper, lower = slice(0, count), slice(count, 2 * count)

    @pl.loop(0, count // STEP)
    def _(step):
        at, below = chunk(step)
        store_folded(one_hi, one_lo, at, [value[a, at, :].astype(jnp.float32) for a in range(BLOCKS)])
        store_folded(one_hi, one_lo, below, [
            grad[a, at, :].astype(jnp.float32) * outer[a, at, :].astype(jnp.float32) for a in range(BLOCKS)])

    for residue in range(BLOCKS):
        spec[residue] = times(one_hi[residue], one_lo[residue], fwd_hi[residue], fwd_lo[residue])
        put(two_hi, two_lo, (residue, upper), multiplied(
            pair(filt, residue, upper), pair(spec, residue, upper), False, residue))
        put(two_hi, two_lo, (residue, lower), multiplied(
            pair(filt, residue, lower), pair(spec, residue, lower), True, residue))
        rows = slice(0, 2 * count)
        back[residue, rows, :] = times(
            two_hi[residue, rows, :], two_lo[residue, rows, :], inv_hi[residue], inv_lo[residue])

    @pl.loop(0, count // STEP)
    def _(step):
        at, below = chunk(step)
        gate = [inner[a, at, :].astype(jnp.float32) for a in range(BLOCKS)]
        inner_act = unfold([pair(back, residue, at) for residue in range(BLOCKS)])
        store_folded(one_hi, one_lo, at, [gate[a] * inner_act[a] for a in range(BLOCKS)])
        grad_mixed = unfold([pair(back, residue, below) for residue in range(BLOCKS)])
        for a in range(BLOCKS):
            grad_inner[a, at, :] = (grad_mixed[a] * inner_act[a]).astype(jnp.bfloat16)
        store_folded(one_hi, one_lo, below, [gate[a] * grad_mixed[a] for a in range(BLOCKS)])

    for residue in range(BLOCKS):
        spec2[...] = times(one_hi[residue], one_lo[residue], fwd_hi[residue], fwd_lo[residue])
        mixed = spec2[upper, :LANES], spec2[upper, LANES:]
        inner_grad = spec2[lower, :LANES], spec2[lower, LANES:]
        products = (
            multiplied(pair(filt, residue, lower), mixed, False, residue),
            multiplied(pair(filt, residue, upper), inner_grad, True, residue),
            multiplied(pair(spec, residue, upper), inner_grad, True, residue),
            multiplied(mixed, pair(spec, residue, lower), True, residue),
        )
        for place, product in enumerate(products):
            put(two_hi, two_lo, (residue, slice(place * count, (place + 1) * count)), product)
        back[residue] = times(two_hi[residue], two_lo[residue], inv_hi[residue], inv_lo[residue])

    @pl.loop(0, count // STEP)
    def _(step):
        def signal(place):
            at = pl.ds(pl.multiple_of(place * count + step * STEP, STEP), STEP)
            return unfold([pair(back, residue, at) for residue in range(BLOCKS)])

        at, below = chunk(step)
        outer_act = signal(0)
        for a in range(BLOCKS):
            grad_outer[a, at, :] = (grad[a, at, :].astype(jnp.float32) * outer_act[a]).astype(jnp.bfloat16)
        value_grad = signal(1)
        for a in range(BLOCKS):
            grad_value[a, at, :] = value_grad[a].astype(jnp.bfloat16)
        for place, rows in ((2, at), (3, below)):
            filter_grad = signal(place)
            window = window_blocks(rate[rows, :])
            for a in range(BLOCKS):
                high, low = halves(filter_grad[a] * window[a])
                lanes = slice(a * LANES, (a + 1) * LANES)
                weighted_hi[rows, lanes] = high
                weighted_lo[rows, lanes] = low

    total = None
    for place, rows in ((0, upper), (1, lower)):
        part = times(weighted_hi[rows, :], weighted_lo[rows, :], feat_hi[place], feat_lo[place])
        total = part if total is None else total + part
    proj_grad[...] = total


def vmem_call(kernel, out_shape, scratch, **extra):
    return pl.pallas_call(
        kernel,
        out_shape=out_shape,
        scratch_shapes=scratch,
        compiler_params=pltpu.CompilerParams(vmem_limit_bytes=56 * 2**20),
        **extra,
    )


def filter_spectra(proj_rows, rates, features, tables):
    count = proj_rows.shape[1]
    twice = proj_rows.reshape(2 * count, -1)
    twice = jnp.concatenate([twice, twice], 1)
    high, low = split_features(features)
    rows = jnp.concatenate([high, low], 1).reshape(BLOCKS, LANES, -1).transpose(0, 2, 1)
    bf, f32 = jnp.bfloat16, jnp.float32
    width = 2 * LANES
    return vmem_call(
        filter_kernel,
        jax.ShapeDtypeStruct((BLOCKS, 2 * count, width), f32),
        [pltpu.VMEM((BLOCKS, 2 * count, LANES), f32)] + [pltpu.VMEM((BLOCKS, 2 * count, width), bf)] * 2,
        name="filter_spectra",
    )(twice, rates.reshape(2 * count, 1), rows, *tables)


def operator_grads(moved, rates, spectra, features, forward, inverse):
    count = moved.shape[1] // 4
    high, low = split_features(features)
    zero = jnp.zeros_like(high)
    placed = [jnp.stack([jnp.concatenate([x, zero], 1), jnp.concatenate([zero, x], 1)]) for x in (high, low)]
    bf, f32 = jnp.bfloat16, jnp.float32
    width = 2 * LANES
    gradients = jax.ShapeDtypeStruct((BLOCKS, 3 * count, LANES), bf)
    return vmem_call(
        main_kernel,
        (gradients, jax.ShapeDtypeStruct((count, 2 * features.shape[1]), f32)),
        [pltpu.VMEM((BLOCKS, 2 * count, width), bf)] * 2
        + [pltpu.VMEM((BLOCKS, 4 * count, width), bf)] * 2
        + [pltpu.VMEM((BLOCKS, 2 * count, width), f32), pltpu.VMEM((2 * count, width), f32),
           pltpu.VMEM((BLOCKS, 4 * count, width), f32)]
        + [pltpu.VMEM((2 * count, BLOCKS * LANES), bf)] * 2,
        name="operator_grads",
    )(moved, rates.reshape(2 * count, 1), spectra, *placed, *forward, *inverse)


highest = lax.Precision.HIGHEST


def angle_table(rows, cols, period):
    row_idx = lax.broadcasted_iota(jnp.int32, (rows, cols), 0)
    col_idx = lax.broadcasted_iota(jnp.int32, (rows, cols), 1)
    angle = (row_idx * col_idx % period).astype(jnp.float32) * (2.0 * math.pi / period)
    return (jnp.cos(angle), jnp.sin(angle))


def split_length(total):
    return max((factor for factor in range(2, math.isqrt(total) + 1, 2) if total % factor == 0))


def forward_dft(signal):
    rows, length = signal.shape
    total = 2 * length
    first = split_length(total)
    second = total // first
    half = first // 2
    shaped = signal.reshape(rows, half, second)
    cos_one, sin_one = angle_table(half, first, first)
    part_re = jnp.einsum("mab,ak->mkb", shaped, cos_one, precision=highest)
    part_im = -jnp.einsum("mab,ak->mkb", shaped, sin_one, precision=highest)
    twist_cos, twist_sin = angle_table(first, second, total)
    turned_re = part_re * twist_cos + part_im * twist_sin
    turned_im = part_im * twist_cos - part_re * twist_sin
    cos_two, sin_two = angle_table(second, second, second)
    out_re = jnp.einsum("mkb,bl->mkl", turned_re, cos_two, precision=highest) + jnp.einsum(
        "mkb,bl->mkl", turned_im, sin_two, precision=highest
    )
    out_im = jnp.einsum("mkb,bl->mkl", turned_im, cos_two, precision=highest) - jnp.einsum(
        "mkb,bl->mkl", turned_re, sin_two, precision=highest
    )
    return (out_re, out_im)


def inverse_dft(spectrum):
    spec_re, spec_im = spectrum
    rows, first, second = spec_re.shape
    total = first * second
    half = first // 2
    cos_two, sin_two = angle_table(second, second, second)
    part_re = jnp.einsum("mkl,lb->mkb", spec_re, cos_two, precision=highest) - jnp.einsum(
        "mkl,lb->mkb", spec_im, sin_two, precision=highest
    )
    part_im = jnp.einsum("mkl,lb->mkb", spec_re, sin_two, precision=highest) + jnp.einsum(
        "mkl,lb->mkb", spec_im, cos_two, precision=highest
    )
    twist_cos, twist_sin = angle_table(first, second, total)
    turned_re = part_re * twist_cos - part_im * twist_sin
    turned_im = part_re * twist_sin + part_im * twist_cos
    cos_one, sin_one = angle_table(half, first, first)
    result = jnp.einsum("mkb,ak->mab", turned_re, cos_one, precision=highest) - jnp.einsum(
        "mkb,ak->mab", turned_im, sin_one, precision=highest
    )
    return result.reshape(rows, half * second) / total


def product_of(left, right, conj_left):
    left_re, left_im = left
    right_re, right_im = right
    if conj_left:
        left_im = -left_im
    return (left_re * right_re - left_im * right_im, left_re * right_im + left_im * right_re)


def rows_of(spectrum, start, count):
    return (spectrum[0][start : start + count], spectrum[1][start : start + count])


def joined(upper, lower):
    return (jnp.concatenate([upper[0], lower[0]], 0), jnp.concatenate([upper[1], lower[1]], 0))


def general_body(value_in, gate_inner, gate_outer, out_grad, filter_proj, decay, frequency):
    seq_pos = lax.axis_index("seq")
    value_cols, inner_cols, outer_cols, grad_cols = (
        lax.all_to_all(value_in, "seq", split_axis=0, concat_axis=1, tiled=True),
        lax.all_to_all(gate_inner, "seq", split_axis=0, concat_axis=1, tiled=True),
        lax.all_to_all(gate_outer, "seq", split_axis=0, concat_axis=1, tiled=True),
        lax.all_to_all(out_grad, "seq", split_axis=0, concat_axis=1, tiled=True),
    )
    count = value_cols.shape[0]
    length = value_cols.shape[1]
    first_row = seq_pos * count
    proj_rows = lax.dynamic_slice_in_dim(filter_proj, first_row, count, 1).astype(jnp.float32)
    rates = lax.dynamic_slice_in_dim(decay, first_row, count, 1)
    positions = lax.iota(jnp.float32, length)
    features = jnp.sin(frequency[None, :] * (positions[:, None] + 1.0))
    window = jnp.sqrt(2.0 * rates)[:, :, None] * jnp.exp(-rates[:, :, None] * positions)
    filters = jnp.einsum("kcf,tf->kct", proj_rows, features, precision=highest) * window
    value_f = value_cols.astype(jnp.float32)
    inner_f = inner_cols.astype(jnp.float32)
    spectra = forward_dft(jnp.concatenate([filters[0], filters[1], value_f], 0))
    inner_spec = rows_of(spectra, 0, count)
    outer_spec = rows_of(spectra, count, count)
    value_spec = rows_of(spectra, 2 * count, count)
    inner_act = inverse_dft(product_of(inner_spec, value_spec, False))
    mixed = inner_f * inner_act
    mixed_spec = forward_dft(mixed)
    outer_act = inverse_dft(product_of(outer_spec, mixed_spec, False))
    outer_f = outer_cols.astype(jnp.float32)
    grad_f = grad_cols.astype(jnp.float32)
    grad_outer = grad_f * outer_act
    grad_spec = forward_dft(grad_f * outer_f)
    outer_back = inverse_dft(
        joined(product_of(outer_spec, grad_spec, True), product_of(mixed_spec, grad_spec, True))
    )
    grad_mixed = outer_back[:count]
    grad_outer_filter = outer_back[count:]
    grad_inner = grad_mixed * inner_act
    inner_grad_spec = forward_dft(grad_mixed * inner_f)
    inner_back = inverse_dft(
        joined(
            product_of(inner_spec, inner_grad_spec, True),
            product_of(value_spec, inner_grad_spec, True),
        )
    )
    grad_value = inner_back[:count]
    grad_inner_filter = inner_back[count:]
    value_out, inner_out, outer_out = (
        lax.all_to_all(
            grad_value.astype(jnp.bfloat16), "seq", split_axis=1, concat_axis=0, tiled=True
        ),
        lax.all_to_all(
            grad_inner.astype(jnp.bfloat16), "seq", split_axis=1, concat_axis=0, tiled=True
        ),
        lax.all_to_all(
            grad_outer.astype(jnp.bfloat16), "seq", split_axis=1, concat_axis=0, tiled=True
        ),
    )
    weighted = jnp.stack([grad_inner_filter, grad_outer_filter]) * window
    own_grad = jnp.einsum("kct,tf->kcf", weighted, features, precision=highest)
    proj_grad = lax.all_gather(own_grad, "seq", axis=1, tiled=True)
    square_sum = lax.psum(jnp.sum(proj_grad * proj_grad), "ch")
    entries = proj_grad.size * lax.axis_size("ch")
    scale = lax.rsqrt(square_sum / entries + 1e-06)
    return (value_out, inner_out, outer_out, proj_grad * scale)


def swapped(x, hop):
    size = lax.axis_size("seq")
    return lax.ppermute(x, "seq", [(i, i ^ hop) for i in range(size)])


def gathered(x):
    place = lax.axis_index("seq")
    hop = BLOCKS // 2
    held = x[None]
    while hop:
        other = swapped(held, hop)
        mine_first = (place & hop) == 0
        held = jnp.where(mine_first, jnp.stack([held, other], 1), jnp.stack([other, held], 1))
        held = held.reshape((-1,) + x.shape)
        hop //= 2
    return held


def body(value_in, gate_inner, gate_outer, out_grad, filter_proj, decay, frequency):
    seq_pos = lax.axis_index("seq")
    channels, lanes = value_in.shape
    count = channels // BLOCKS
    length = BLOCKS * lanes
    forward, inverse = ([jnp.asarray(part) for part in split_table(table)] for table in class_tables())
    proj_rows = lax.dynamic_slice_in_dim(filter_proj, seq_pos * count, count, 1)
    rates = lax.dynamic_slice_in_dim(decay, seq_pos * count, count, 1)
    features = jnp.sin(frequency[None, :] * (lax.iota(jnp.float32, length)[:, None] + 1.0))
    spectra = filter_spectra(proj_rows, rates, features, forward)
    stacked = jnp.concatenate(
        [x.reshape(BLOCKS, count, lanes) for x in (value_in, gate_inner, gate_outer, out_grad)], 1
    )
    moved = lax.all_to_all(stacked, "seq", split_axis=0, concat_axis=0, tiled=True)
    grads, own_grad = operator_grads(moved, rates, spectra, features, forward, inverse)
    back = lax.all_to_all(grads, "seq", split_axis=0, concat_axis=0, tiled=True)
    outs = [back[:, i * count : (i + 1) * count].reshape(channels, lanes) for i in range(3)]
    proj_grad = gathered(own_grad)
    square_sum = jnp.sum(proj_grad * proj_grad)
    for hop in (1, 2):
        square_sum = square_sum + lax.ppermute(square_sum, "ch", [(i, i ^ hop) for i in range(4)])
    scale = lax.rsqrt(square_sum / (proj_grad.size * 4) + 1e-06)
    both = proj_grad.reshape(channels, 2, -1).transpose(1, 0, 2)
    return (*outs, both * scale)


def solution(mesh):
    def chosen(*arrays):
        whole = arrays[0].shape[1] == LANES and arrays[0].shape[0] % (BLOCKS * STEP) == 0
        fits = lax.axis_size("seq") == BLOCKS and lax.axis_size("ch") == 4
        return body(*arrays) if whole and fits else general_body(*arrays)

    split = P("ch", "seq")
    rows = P(None, "ch", None)
    return jax.shard_map(
        chosen,
        mesh=mesh,
        in_specs=(split, split, split, split, rows, P(None, "ch"), P()),
        out_specs=(split, split, split, rows),
        check_vma=False,
    )
```

```python
import math
import functools
import numpy as np
import ml_dtypes
import jax
import jax.numpy as jnp
from jax import lax
from jax.experimental import pallas as pl
from jax.experimental.pallas import tpu as pltpu
from jax.sharding import PartitionSpec as P

BLOCKS = 8
LANES = 128
COS1, COS2, COS3 = (math.cos(math.pi / 8), math.cos(math.pi / 4), math.cos(3 * math.pi / 8))
STEP = 16
SENT, RETURNED = 3, 4
LIMIT = 60
PRODUCT_SCALE, OUTER_SCALE = 2.0**24, 2.0**-3


def class_zero():
    points = BLOCKS * LANES * 2
    lane = np.arange(LANES)
    half = LANES // 2
    forward = np.zeros((2 * LANES, 2 * LANES))
    for offset, first, rows in ((0, 0, slice(0, LANES)), (8, half, slice(LANES, 2 * LANES))):
        angle = 2 * np.pi * np.outer(lane, 16 * lane[:half] + offset) / points
        forward[rows, first : first + half] = np.cos(angle)
        forward[rows, LANES + first : LANES + first + half] = -np.sin(angle)
    forward[:LANES, LANES] = (-1.0) ** lane
    inverse = forward.T.copy()
    inverse[[0, LANES]] *= 0.5
    parts = []
    for table in (forward, inverse):
        high = table.astype(ml_dtypes.bfloat16)
        parts += [high, (table - high.astype(np.float64)).astype(ml_dtypes.bfloat16)]
    return np.stack(parts)


def angles():
    lane = np.arange(LANES)
    whole = 2 * np.pi * np.outer(lane, lane) / LANES
    turn = 2 * np.pi * np.outer(lane, lane) / (2 * BLOCKS * LANES)
    return np.stack([np.cos(whole), np.sin(whole), np.cos(turn), np.sin(turn)]).astype(np.float32)


def fold(x):
    s = [x[a] + x[a + 4] for a in range(4)]
    d = [x[a] - x[a + 4] for a in range(4)]
    t0, t1 = s[0] + s[2], s[1] + s[3]
    u0, u1 = s[0] - s[2], s[1] - s[3]
    p, w = (d[1] - d[3]) * COS2, (d[1] + d[3]) * COS2
    p1, p2, p3 = x[1] - x[7], (x[2] - x[6]) * COS2, x[3] - x[5]
    n1, n2, n3 = x[1] + x[7], (x[2] + x[6]) * COS2, x[3] + x[5]
    a0, b0 = x[0] + p2, x[0] - p2
    c0, d0 = p1 * COS1 + p3 * COS3, p1 * COS3 - p3 * COS1
    a1, b1 = n2 + x[4], n2 - x[4]
    c1, d1 = n1 * COS3 + n3 * COS1, n1 * COS1 - n3 * COS3
    return (
        (t0 + t1, t0 - t1),
        (a0 + c0, c1 + a1),
        (d[0] + p, d[2] + w),
        (b0 + d0, d1 + b1),
        (u0, u1),
        (b0 - d0, d1 - b1),
        (d[0] - p, w - d[2]),
        (a0 - c0, c1 - a1),
    )


def unfold(z):
    (z0, z8), (r1, i1), (r2, i2), (r3, i3), (r4, i4), (r5, i5), (r6, i6), (r7, i7) = z
    even, odd = z0 + z8, z0 - z8
    g = [even + r4, odd + i4, even - r4, odd - i4]
    dr, di = r2 - r6, i2 + i6
    h = [r2 + r6, (dr + di) * COS2, i2 - i6, (di - dr) * COS2]
    rs, rd, ts, td = r1 + r7, r1 - r7, r3 + r5, r3 - r5
    js, jd, ks, kd = i1 + i7, i1 - i7, i3 + i5, i3 - i5
    k = [None, rd * COS1 + td * COS3, (rs - ts) * COS2, rd * COS3 - td * COS1]
    m = [None, js * COS3 + ks * COS1, (jd + kd) * COS2, js * COS1 - ks * COS3]
    o = [rs + ts, k[1] + m[1], k[2] + m[2], k[3] + m[3], jd - kd, m[3] - k[3], m[2] - k[2], m[1] - k[1]]
    return [g[a] + h[a] + o[a] for a in range(4)] + [g[a] - h[a] + o[a + 4] for a in range(4)]


def fourth_power(x, scale):
    x = x * scale
    return (x * x * (x * jnp.abs(x))).astype(jnp.bfloat16)


def fourth_root(code, scale):
    code = code.astype(jnp.float32)
    size = jnp.sqrt(jnp.sqrt(jnp.abs(code))) * (1.0 / scale)
    return jnp.where(code < 0, -size, size)


def halves(x):
    high = x.astype(jnp.bfloat16)
    return high, (x - high.astype(jnp.float32)).astype(jnp.bfloat16)


def split_features(features):
    high = lax.reduce_precision(features, 8, 7)
    return high.astype(jnp.bfloat16), (features - high).astype(jnp.bfloat16)


def put(hi_ref, lo_ref, index, parts):
    for part, x in enumerate(parts):
        high, low = halves(x)
        lanes = slice(part * LANES, (part + 1) * LANES)
        hi_ref[index + (lanes,)] = high
        lo_ref[index + (lanes,)] = low


def store_folded(hi_ref, lo_ref, rows, blocks):
    for residue, parts in enumerate(fold(blocks)):
        put(hi_ref, lo_ref, (residue, rows), parts)


def make_table(angle, residue, table_hi, table_lo):
    cos, sin = angle[0], angle[1]
    turn_cos, turn_sin = angle[2, :, residue : residue + 1], angle[3, :, residue : residue + 1]
    real = cos * turn_cos - sin * turn_sin
    imag = -(sin * turn_cos + cos * turn_sin)
    left, right = slice(0, LANES), slice(LANES, 2 * LANES)
    for (rows, lanes), x in (((left, left), real), ((left, right), imag), ((right, left), imag), ((right, right), -real)):
        high, low = halves(x)
        table_hi[residue, rows, lanes] = high
        table_lo[residue, rows, lanes] = low


def times_transposed(high, low, table_hi, table_lo):
    def dot(x, table):
        return lax.dot_general(x, table, (((1,), (1,)), ((), ())), preferred_element_type=jnp.float32)

    return dot(high, table_hi) + (dot(low, table_hi) + dot(high, table_lo))


def times(high, low, table_hi, table_lo):
    dot = functools.partial(jnp.dot, preferred_element_type=jnp.float32)
    return dot(high, table_hi) + (dot(low, table_hi) + dot(high, table_lo))


def multiplied(left, right, conj, residue):
    a_re, a_im = left
    b_re, b_im = right
    rr, ii, ri, ir = a_re * b_re, a_im * b_im, a_re * b_im, a_im * b_re
    if conj:
        re, im = rr + ii, ri - ir
    else:
        re, im = rr - ii, ri + ir
    if residue == 0:
        shared = lax.broadcasted_iota(jnp.int32, re.shape, 1) == 0
        re, im = jnp.where(shared, rr, re), jnp.where(shared, ii, im)
    return re, im


def window_blocks(rate):
    rate = jnp.broadcast_to(rate, (rate.shape[0], LANES))
    place = lax.broadcasted_iota(jnp.int32, rate.shape, 1).astype(jnp.float32)
    first = jnp.sqrt(2.0 * rate) * jnp.exp(-rate * place) * (1.0 / (BLOCKS * LANES))
    return [first * jnp.exp(rate * (-float(LANES) * a)) if a else first for a in range(BLOCKS)]


def fetched(sources, places, sems):
    copies = [pltpu.make_async_copy(src, dst, sems.at[i]) for i, (src, dst) in enumerate(zip(sources, places))]
    for copy in copies:
        copy.start()
    return copies


def filter_kernel(proj, rate, features, angle, zero, spectra, filters, fold_hi, fold_lo, table_hi, table_lo):
    rows = proj.shape[0]
    for a in range(BLOCKS):
        filters[a] = jnp.dot(proj[...], features[a], preferred_element_type=jnp.float32)

    @pl.loop(0, rows // STEP)
    def _(step):
        at = pl.ds(pl.multiple_of(step * STEP, STEP), STEP)
        window = window_blocks(rate[at, :])
        store_folded(fold_hi, fold_lo, at, [filters[a, at, :] * window[a] for a in range(BLOCKS)])

    spectra[0] = times(fold_hi[0], fold_lo[0], zero[0], zero[1])
    for residue in range(1, BLOCKS):
        make_table(angle, residue, table_hi, table_lo)
        spectra[residue] = times(fold_hi[residue], fold_lo[residue], table_hi[residue], table_lo[residue])


def main_kernel(
    moved, rate, filt, angle, zero, features,
    results,
    one_hi, one_lo, two_hi, two_lo, spec, spec2, back, weighted_hi, weighted_lo, table_hi, table_lo,
):
    count = moved.shape[1] // SENT
    value, inner, product = (moved.at[:, i * count : (i + 1) * count] for i in range(SENT))
    grad_value, grad_inner, outer_coded = (results.at[:, i * count : (i + 1) * count] for i in range(3))
    def forward(residue):
        tables = (table_hi[residue], table_lo[residue]) if residue else (zero[0], zero[1])
        return times(one_hi[residue], one_lo[residue], *tables)

    def inverse(residue, rows):
        high, low = two_hi[residue, rows, :], two_lo[residue, rows, :]
        if residue:
            return times_transposed(high, low, table_hi[residue], table_lo[residue])
        return times(high, low, zero[2], zero[3])

    def chunk(step):
        return pl.ds(pl.multiple_of(step * STEP, STEP), STEP), pl.ds(pl.multiple_of(count + step * STEP, STEP), STEP)

    def pair(ref, residue, rows):
        return ref[residue, rows, :LANES], ref[residue, rows, LANES:]

    upper, lower = slice(0, count), slice(count, 2 * count)

    @pl.loop(0, count // STEP)
    def _(step):
        at, below = chunk(step)
        store_folded(one_hi, one_lo, at, [value[a, at, :].astype(jnp.float32) for a in range(BLOCKS)])
        store_folded(one_hi, one_lo, below, [fourth_root(product[a, at, :], PRODUCT_SCALE) for a in range(BLOCKS)])

    for residue in range(BLOCKS):
        if residue:
            make_table(angle, residue, table_hi, table_lo)
        spec[residue] = forward(residue)
        put(two_hi, two_lo, (residue, upper), multiplied(
            pair(filt, residue, upper), pair(spec, residue, upper), False, residue))
        put(two_hi, two_lo, (residue, lower), multiplied(
            pair(filt, residue, lower), pair(spec, residue, lower), True, residue))
        rows = slice(0, 2 * count)
        back[residue, rows, :] = inverse(residue, rows)

    @pl.loop(0, count // STEP)
    def _(step):
        at, below = chunk(step)
        gate = [inner[a, at, :].astype(jnp.float32) for a in range(BLOCKS)]
        inner_act = unfold([pair(back, residue, at) for residue in range(BLOCKS)])
        store_folded(one_hi, one_lo, at, [gate[a] * inner_act[a] for a in range(BLOCKS)])
        grad_mixed = unfold([pair(back, residue, below) for residue in range(BLOCKS)])
        for a in range(BLOCKS):
            grad_inner[a, at, :] = (grad_mixed[a] * inner_act[a]).astype(jnp.bfloat16)
        store_folded(one_hi, one_lo, below, [gate[a] * grad_mixed[a] for a in range(BLOCKS)])

    for residue in range(BLOCKS):
        spec2[...] = forward(residue)
        mixed = spec2[upper, :LANES], spec2[upper, LANES:]
        inner_grad = spec2[lower, :LANES], spec2[lower, LANES:]
        products = (
            multiplied(pair(filt, residue, lower), mixed, False, residue),
            multiplied(pair(filt, residue, upper), inner_grad, True, residue),
            multiplied(pair(spec, residue, upper), inner_grad, True, residue),
            multiplied(mixed, pair(spec, residue, lower), True, residue),
        )
        for place, product in enumerate(products):
            put(two_hi, two_lo, (residue, slice(place * count, (place + 1) * count)), product)
        back[residue] = inverse(residue, slice(0, 4 * count))

    @pl.loop(0, count // STEP)
    def _(step):
        def signal(place):
            at = pl.ds(pl.multiple_of(place * count + step * STEP, STEP), STEP)
            return unfold([pair(back, residue, at) for residue in range(BLOCKS)])

        at, below = chunk(step)
        outer_act = signal(0)
        for a in range(BLOCKS):
            outer_coded[a, at, :] = fourth_power(outer_act[a], OUTER_SCALE)
        value_grad = signal(1)
        for a in range(BLOCKS):
            grad_value[a, at, :] = value_grad[a].astype(jnp.bfloat16)
        for place, rows in ((2, at), (3, below)):
            filter_grad = signal(place)
            window = window_blocks(rate[rows, :])
            for a in range(BLOCKS):
                high, low = halves(filter_grad[a] * window[a])
                lanes = slice(a * LANES, (a + 1) * LANES)
                weighted_hi[rows, lanes] = high
                weighted_lo[rows, lanes] = low

    dot = functools.partial(jnp.dot, preferred_element_type=jnp.float32)
    total = (dot(weighted_hi[...], features[...]) + dot(weighted_lo[...], features[...])).T
    half = total.shape[0] // 2
    total = total[:half] + total[half:]
    for place in range(2):
        part = total[:, place * count : (place + 1) * count]
        coded = (part * jnp.abs(part)).astype(jnp.bfloat16)
        for a in range(BLOCKS):
            results[a, 3 * count + place * half : 3 * count + (place + 1) * half] = coded


def device_call(kernel, out_shape, scratch, in_vmem, out_vmem, name, limit):
    def spec(inside):
        return pl.BlockSpec(memory_space=pltpu.VMEM if inside else pl.ANY)

    return pl.pallas_call(
        kernel,
        out_shape=out_shape,
        in_specs=[spec(inside) for inside in in_vmem],
        out_specs=[spec(inside) for inside in out_vmem],
        scratch_shapes=scratch,
        compiler_params=pltpu.CompilerParams(vmem_limit_bytes=limit * 2**20),
        name=name,
    )


def filter_spectra(proj_rows, rates, terms, angle, zero):
    rows = proj_rows.shape[0]
    twice = jnp.concatenate([proj_rows, proj_rows], 1)
    terms = terms.reshape(BLOCKS, LANES, -1).transpose(0, 2, 1)
    bf, f32 = jnp.bfloat16, jnp.float32
    width = 2 * LANES
    return device_call(
        filter_kernel,
        [jax.ShapeDtypeStruct((BLOCKS, rows, width), f32)],
        [pltpu.VMEM((BLOCKS, rows, LANES), f32)]
        + [pltpu.VMEM((BLOCKS, rows, width), bf)] * 2
        + [pltpu.VMEM((BLOCKS, width, width), bf)] * 2,
        (True,) * 5,
        (True,),
        "filter_spectra",
        16,
    )(twice, rates.reshape(rows, 1), terms, angle, zero)[0]


def operator_grads(moved, rates, spectra, angle, zero, terms):
    count = moved.shape[1] // SENT
    bf, f32 = jnp.bfloat16, jnp.float32
    width = 2 * LANES
    return device_call(
        main_kernel,
        [jax.ShapeDtypeStruct((BLOCKS, RETURNED * count, LANES), bf)],
        [pltpu.VMEM((BLOCKS, 2 * count, width), bf)] * 2
        + [pltpu.VMEM((BLOCKS, 4 * count, width), bf)] * 2
        + [pltpu.VMEM((BLOCKS, 2 * count, width), f32), pltpu.VMEM((2 * count, width), f32),
           pltpu.VMEM((BLOCKS, 4 * count, width), f32)]
        + [pltpu.VMEM((2 * count, BLOCKS * LANES), bf)] * 2
        + [pltpu.VMEM((BLOCKS, width, width), bf)] * 2,
        (True,) * 6,
        (True,),
        "operator_grads",
        32,
    )(moved, rates.reshape(2 * count, 1), spectra, angle, zero, terms)[0]


def pack_kernel(value, inner, outer, grad, sent, outer_in, grad_in, sems):
    count = sent.shape[1] // SENT
    copies = fetched(
        (outer, grad, value, inner),
        (outer_in, grad_in, sent.at[:, :count], sent.at[:, count : 2 * count]),
        sems,
    )
    for copy in copies[:2]:
        copy.wait()
    for a in range(BLOCKS):
        both = grad_in[a].astype(jnp.float32) * outer_in[a].astype(jnp.float32)
        sent[a, 2 * count :] = fourth_power(both, PRODUCT_SCALE)
    for copy in copies[2:]:
        copy.wait()


def packed(*arrays):
    channels, lanes = arrays[0].shape
    count = channels // BLOCKS
    block = pltpu.VMEM((BLOCKS, count, lanes), jnp.bfloat16)
    return device_call(
        pack_kernel,
        [jax.ShapeDtypeStruct((BLOCKS, SENT * count, lanes), jnp.bfloat16)],
        [block, block, pltpu.SemaphoreType.DMA((4,))],
        (False,) * 4,
        (True,),
        "packed",
        LIMIT,
    )(*(x.reshape(BLOCKS, count, lanes) for x in arrays))[0]


def sum_kernel(back, total):
    first = 3 * (back.shape[1] // RETURNED)
    part = jnp.zeros(total.shape, jnp.float32)
    for a in range(BLOCKS):
        size = jnp.abs(back[a, first:].astype(jnp.float32))
        part = part + jnp.sum(size.reshape((-1,) + total.shape), 0)
    total[...] = jnp.broadcast_to(jnp.sum(part, keepdims=True), total.shape)


def square_total(back):
    return device_call(
        sum_kernel, [jax.ShapeDtypeStruct((8, LANES), jnp.float32)], [], (True,), (True,), "square_total", 16
    )(back)[0]


def unpack_kernel(back, grad, grad_value, grad_inner, grad_outer, grad_in, outer_out, sems):
    count = back.shape[1] // RETURNED
    copies = fetched(
        (grad, back.at[:, :count], back.at[:, count : 2 * count]), (grad_in, grad_value, grad_inner), sems
    )
    copies[0].wait()
    for a in range(BLOCKS):
        act = fourth_root(back[a, 2 * count : 3 * count], OUTER_SCALE)
        outer_out[a] = (grad_in[a].astype(jnp.float32) * act).astype(jnp.bfloat16)
    last = pltpu.make_async_copy(outer_out, grad_outer, sems.at[3])
    last.start()
    for copy in (*copies[1:], last):
        copy.wait()


def unpacked(back, grad):
    channels, lanes = grad.shape
    count = channels // BLOCKS
    block = jax.ShapeDtypeStruct((BLOCKS, count, lanes), jnp.bfloat16)
    held = pltpu.VMEM(block.shape, block.dtype)
    grads = device_call(
        unpack_kernel,
        [block] * 3,
        [held, held, pltpu.SemaphoreType.DMA((4,))],
        (True, False),
        (False,) * 3,
        "unpacked",
        16,
    )(back, grad.reshape(block.shape))
    return [x.reshape(channels, lanes) for x in grads]


def scale_kernel(entries, back, one, two, three, four, out, held, sem):
    count = back.shape[1] // RETURNED
    mean = (one[...] + two[...] + three[...] + four[...]) * (1.0 / entries) + 1e-06
    scale = lax.rsqrt(mean)[:1]
    features = held.shape[1]
    for a in range(BLOCKS):
        for place in range(2):
            first = 3 * count + place * features
            coded = back[a, first : first + features].astype(jnp.float32)
            size = jnp.sqrt(jnp.abs(coded)) * scale
            held[place, :, a * LANES : (a + 1) * LANES] = jnp.where(coded < 0, -size, size)
    copy = pltpu.make_async_copy(held, out, sem)
    copy.start()
    copy.wait()


def scaled(back, sums, entries, features):
    shape = (2, features, BLOCKS * LANES)
    return device_call(
        functools.partial(scale_kernel, entries),
        [jax.ShapeDtypeStruct(shape, jnp.float32)],
        [pltpu.VMEM(shape, jnp.float32), pltpu.SemaphoreType.DMA],
        (True,) * 5,
        (False,),
        "scaled",
        16,
    )(back, *sums)[0]


highest = lax.Precision.HIGHEST


def angle_table(rows, cols, period):
    row_idx = lax.broadcasted_iota(jnp.int32, (rows, cols), 0)
    col_idx = lax.broadcasted_iota(jnp.int32, (rows, cols), 1)
    angle = (row_idx * col_idx % period).astype(jnp.float32) * (2.0 * math.pi / period)
    return (jnp.cos(angle), jnp.sin(angle))


def split_length(total):
    return max((factor for factor in range(2, math.isqrt(total) + 1, 2) if total % factor == 0))


def forward_dft(signal):
    rows, length = signal.shape
    total = 2 * length
    first = split_length(total)
    second = total // first
    half = first // 2
    shaped = signal.reshape(rows, half, second)
    cos_one, sin_one = angle_table(half, first, first)
    part_re = jnp.einsum("mab,ak->mkb", shaped, cos_one, precision=highest)
    part_im = -jnp.einsum("mab,ak->mkb", shaped, sin_one, precision=highest)
    twist_cos, twist_sin = angle_table(first, second, total)
    turned_re = part_re * twist_cos + part_im * twist_sin
    turned_im = part_im * twist_cos - part_re * twist_sin
    cos_two, sin_two = angle_table(second, second, second)
    out_re = jnp.einsum("mkb,bl->mkl", turned_re, cos_two, precision=highest) + jnp.einsum(
        "mkb,bl->mkl", turned_im, sin_two, precision=highest
    )
    out_im = jnp.einsum("mkb,bl->mkl", turned_im, cos_two, precision=highest) - jnp.einsum(
        "mkb,bl->mkl", turned_re, sin_two, precision=highest
    )
    return (out_re, out_im)


def inverse_dft(spectrum):
    spec_re, spec_im = spectrum
    rows, first, second = spec_re.shape
    total = first * second
    half = first // 2
    cos_two, sin_two = angle_table(second, second, second)
    part_re = jnp.einsum("mkl,lb->mkb", spec_re, cos_two, precision=highest) - jnp.einsum(
        "mkl,lb->mkb", spec_im, sin_two, precision=highest
    )
    part_im = jnp.einsum("mkl,lb->mkb", spec_re, sin_two, precision=highest) + jnp.einsum(
        "mkl,lb->mkb", spec_im, cos_two, precision=highest
    )
    twist_cos, twist_sin = angle_table(first, second, total)
    turned_re = part_re * twist_cos - part_im * twist_sin
    turned_im = part_re * twist_sin + part_im * twist_cos
    cos_one, sin_one = angle_table(half, first, first)
    result = jnp.einsum("mkb,ak->mab", turned_re, cos_one, precision=highest) - jnp.einsum(
        "mkb,ak->mab", turned_im, sin_one, precision=highest
    )
    return result.reshape(rows, half * second) / total


def product_of(left, right, conj_left):
    left_re, left_im = left
    right_re, right_im = right
    if conj_left:
        left_im = -left_im
    return (left_re * right_re - left_im * right_im, left_re * right_im + left_im * right_re)


def rows_of(spectrum, start, count):
    return (spectrum[0][start : start + count], spectrum[1][start : start + count])


def joined(upper, lower):
    return (jnp.concatenate([upper[0], lower[0]], 0), jnp.concatenate([upper[1], lower[1]], 0))


def general_body(value_in, gate_inner, gate_outer, out_grad, filter_proj, decay, frequency):
    seq_pos = lax.axis_index("seq")
    value_cols, inner_cols, outer_cols, grad_cols = (
        lax.all_to_all(value_in, "seq", split_axis=0, concat_axis=1, tiled=True),
        lax.all_to_all(gate_inner, "seq", split_axis=0, concat_axis=1, tiled=True),
        lax.all_to_all(gate_outer, "seq", split_axis=0, concat_axis=1, tiled=True),
        lax.all_to_all(out_grad, "seq", split_axis=0, concat_axis=1, tiled=True),
    )
    count = value_cols.shape[0]
    length = value_cols.shape[1]
    first_row = seq_pos * count
    proj_rows = lax.dynamic_slice_in_dim(filter_proj, first_row, count, 1).astype(jnp.float32)
    rates = lax.dynamic_slice_in_dim(decay, first_row, count, 1)
    positions = lax.iota(jnp.float32, length)
    features = jnp.sin(frequency[None, :] * (positions[:, None] + 1.0))
    window = jnp.sqrt(2.0 * rates)[:, :, None] * jnp.exp(-rates[:, :, None] * positions)
    filters = jnp.einsum("kcf,tf->kct", proj_rows, features, precision=highest) * window
    value_f = value_cols.astype(jnp.float32)
    inner_f = inner_cols.astype(jnp.float32)
    spectra = forward_dft(jnp.concatenate([filters[0], filters[1], value_f], 0))
    inner_spec = rows_of(spectra, 0, count)
    outer_spec = rows_of(spectra, count, count)
    value_spec = rows_of(spectra, 2 * count, count)
    inner_act = inverse_dft(product_of(inner_spec, value_spec, False))
    mixed = inner_f * inner_act
    mixed_spec = forward_dft(mixed)
    outer_act = inverse_dft(product_of(outer_spec, mixed_spec, False))
    outer_f = outer_cols.astype(jnp.float32)
    grad_f = grad_cols.astype(jnp.float32)
    grad_outer = grad_f * outer_act
    grad_spec = forward_dft(grad_f * outer_f)
    outer_back = inverse_dft(
        joined(product_of(outer_spec, grad_spec, True), product_of(mixed_spec, grad_spec, True))
    )
    grad_mixed = outer_back[:count]
    grad_outer_filter = outer_back[count:]
    grad_inner = grad_mixed * inner_act
    inner_grad_spec = forward_dft(grad_mixed * inner_f)
    inner_back = inverse_dft(
        joined(
            product_of(inner_spec, inner_grad_spec, True),
            product_of(value_spec, inner_grad_spec, True),
        )
    )
    grad_value = inner_back[:count]
    grad_inner_filter = inner_back[count:]
    value_out, inner_out, outer_out = (
        lax.all_to_all(
            grad_value.astype(jnp.bfloat16), "seq", split_axis=1, concat_axis=0, tiled=True
        ),
        lax.all_to_all(
            grad_inner.astype(jnp.bfloat16), "seq", split_axis=1, concat_axis=0, tiled=True
        ),
        lax.all_to_all(
            grad_outer.astype(jnp.bfloat16), "seq", split_axis=1, concat_axis=0, tiled=True
        ),
    )
    weighted = jnp.stack([grad_inner_filter, grad_outer_filter]) * window
    own_grad = jnp.einsum("kct,tf->kcf", weighted, features, precision=highest)
    proj_grad = lax.all_gather(own_grad, "seq", axis=1, tiled=True)
    square_sum = lax.psum(jnp.sum(proj_grad * proj_grad), "ch")
    entries = proj_grad.size * lax.axis_size("ch")
    scale = lax.rsqrt(square_sum / entries + 1e-06)
    return (value_out, inner_out, outer_out, proj_grad * scale)


def body(value_in, gate_inner, gate_outer, out_grad, filter_proj, decay, frequency):
    seq_pos = lax.axis_index("seq")
    channels, lanes = value_in.shape
    count = channels // BLOCKS
    length = BLOCKS * lanes
    angle, zero = jnp.asarray(angles()), jnp.asarray(class_zero())

    def own_rows(x):
        rows = lax.dynamic_slice_in_dim(x, seq_pos * count, count, 1)
        return rows.reshape((2 * count,) + x.shape[2:])

    sent = packed(value_in, gate_inner, gate_outer, out_grad)
    moved = lax.all_to_all(sent, "seq", split_axis=0, concat_axis=0, tiled=True)
    rates = own_rows(decay)
    features = jnp.sin(frequency[None, :] * (lax.iota(jnp.float32, length)[:, None] + 1.0))
    terms = jnp.concatenate(split_features(features), 1)
    spectra = filter_spectra(own_rows(filter_proj), rates, terms, angle, zero)
    results = operator_grads(moved, rates, spectra, angle, zero, terms)
    back = lax.all_to_all(results, "seq", split_axis=0, concat_axis=0, tiled=True)
    own_sum = square_total(back)
    groups = lax.axis_size("ch")
    sums = [own_sum] + [
        lax.ppermute(own_sum, "ch", [(i, i ^ hop) for i in range(groups)]) for hop in range(1, groups)
    ]
    grads = unpacked(back, out_grad)
    proj_grad = scaled(back, sums, filter_proj.size * groups, features.shape[1])
    return (*grads, proj_grad.transpose(0, 2, 1))


def solution(mesh):
    def chosen(*arrays):
        whole = arrays[0].shape[1] == LANES and arrays[0].shape[0] % (BLOCKS * STEP) == 0
        fits = lax.axis_size("seq") == BLOCKS and lax.axis_size("ch") == 4
        return body(*arrays) if whole and fits else general_body(*arrays)

    split = P("ch", "seq")
    rows = P(None, "ch", None)
    return jax.shard_map(
        chosen,
        mesh=mesh,
        in_specs=(split, split, split, split, rows, P(None, "ch"), P()),
        out_specs=(split, split, split, rows),
        check_vma=False,
    )
```

```python
import math
import functools
import numpy as np
import ml_dtypes
import jax
import jax.numpy as jnp
from jax import lax
from jax.experimental import pallas as pl
from jax.experimental.pallas import tpu as pltpu
from jax.sharding import PartitionSpec as P

BLOCKS = 8
LANES = 128
COS1, COS2, COS3 = (math.cos(math.pi / 8), math.cos(math.pi / 4), math.cos(3 * math.pi / 8))
STEP = 16
SIN_AT, SIGN_AT = 16, 32
PEERS = (1, 4, 2, 6, 3, 5, 7)
SENT, RETURNED = 3, 4
PACK_LIMIT, MAIN_LIMIT = 60, 32
PRODUCT_SCALE, OUTER_SCALE = 2.0**24, 2.0**-3


def angles():
    lane = np.arange(LANES)
    whole = 2 * np.pi * np.outer(lane, lane) / LANES
    turn = 2 * np.pi * np.outer(lane, np.arange(BLOCKS + 1)) / (2 * BLOCKS * LANES)
    turn[:, BLOCKS] += np.pi * lane
    columns = np.zeros((LANES, LANES))
    columns[:, : BLOCKS + 1] = np.cos(turn)
    columns[:, SIN_AT : SIN_AT + BLOCKS + 1] = np.sin(turn)
    columns[:, SIGN_AT] = 1.0 - 2.0 * (lane % 2)
    return np.stack([np.cos(whole), np.sin(whole), columns]).astype(np.float32)


def fold(x):
    s = [x[a] + x[a + 4] for a in range(4)]
    d = [x[a] - x[a + 4] for a in range(4)]
    t0, t1 = s[0] + s[2], s[1] + s[3]
    u0, u1 = s[0] - s[2], s[1] - s[3]
    p, w = (d[1] - d[3]) * COS2, (d[1] + d[3]) * COS2
    p1, p2, p3 = x[1] - x[7], (x[2] - x[6]) * COS2, x[3] - x[5]
    n1, n2, n3 = x[1] + x[7], (x[2] + x[6]) * COS2, x[3] + x[5]
    a0, b0 = x[0] + p2, x[0] - p2
    c0, d0 = p1 * COS1 + p3 * COS3, p1 * COS3 - p3 * COS1
    a1, b1 = n2 + x[4], n2 - x[4]
    c1, d1 = n1 * COS3 + n3 * COS1, n1 * COS1 - n3 * COS3
    return (
        (t0 + t1, t0 - t1),
        (a0 + c0, c1 + a1),
        (d[0] + p, d[2] + w),
        (b0 + d0, d1 + b1),
        (u0, u1),
        (b0 - d0, d1 - b1),
        (d[0] - p, w - d[2]),
        (a0 - c0, c1 - a1),
    )


def unfold(z):
    (z0, z8), (r1, i1), (r2, i2), (r3, i3), (r4, i4), (r5, i5), (r6, i6), (r7, i7) = z
    even, odd = z0 + z8, z0 - z8
    g = [even + r4, odd + i4, even - r4, odd - i4]
    dr, di = r2 - r6, i2 + i6
    h = [r2 + r6, (dr + di) * COS2, i2 - i6, (di - dr) * COS2]
    rs, rd, ts, td = r1 + r7, r1 - r7, r3 + r5, r3 - r5
    js, jd, ks, kd = i1 + i7, i1 - i7, i3 + i5, i3 - i5
    k = [None, rd * COS1 + td * COS3, (rs - ts) * COS2, rd * COS3 - td * COS1]
    m = [None, js * COS3 + ks * COS1, (jd + kd) * COS2, js * COS1 - ks * COS3]
    o = [rs + ts, k[1] + m[1], k[2] + m[2], k[3] + m[3], jd - kd, m[3] - k[3], m[2] - k[2], m[1] - k[1]]
    return [g[a] + h[a] + o[a] for a in range(4)] + [g[a] - h[a] + o[a + 4] for a in range(4)]


def fourth_power(x, scale):
    x = x * scale
    return (x * x * (x * jnp.abs(x))).astype(jnp.bfloat16)


def fourth_root(code, scale):
    code = code.astype(jnp.float32)
    size = jnp.sqrt(jnp.sqrt(jnp.abs(code))) * (1.0 / scale)
    return jnp.where(code < 0, -size, size)


def halves(x):
    high = x.astype(jnp.bfloat16)
    return high, (x - high.astype(jnp.float32)).astype(jnp.bfloat16)


def split_features(features):
    high = lax.reduce_precision(features, 8, 7)
    return high.astype(jnp.bfloat16), (features - high).astype(jnp.bfloat16)


def put(hi_ref, lo_ref, index, parts):
    for part, x in enumerate(parts):
        high, low = halves(x)
        lanes = slice(part * LANES, (part + 1) * LANES)
        hi_ref[index + (lanes,)] = high
        lo_ref[index + (lanes,)] = low


def store_folded(hi_ref, lo_ref, rows, blocks):
    for residue, parts in enumerate(fold(blocks)):
        put(hi_ref, lo_ref, (residue, rows), parts)


def make_table(angle, residue, table_hi, table_lo):
    def turned(column):
        cos, sin = angle[0], angle[1]
        turn_cos, turn_sin = angle[2, :, column : column + 1], angle[2, :, SIN_AT + column : SIN_AT + column + 1]
        return cos * turn_cos - sin * turn_sin, -(sin * turn_cos + cos * turn_sin)

    real, imag = turned(residue)
    if residue:
        blocks = ((real, imag), (imag, -real))
    else:
        lane = lax.broadcasted_iota(jnp.int32, real.shape, 1)
        below = lane < LANES // 2
        sign = jnp.broadcast_to(angle[2, :, SIGN_AT : SIGN_AT + 1], real.shape)
        top = jnp.where(below, real, 0.0), jnp.where(lane == 0, sign, jnp.where(below, imag, 0.0))
        blocks = (top, tuple(jnp.where(below, 0.0, x) for x in turned(BLOCKS)))
    for i, row in enumerate(blocks):
        for j, x in enumerate(row):
            high, low = halves(x)
            at = residue, slice(i * LANES, (i + 1) * LANES), slice(j * LANES, (j + 1) * LANES)
            table_hi[at] = high
            table_lo[at] = low


def times_transposed(high, low, table_hi, table_lo):
    def dot(x, table):
        return lax.dot_general(x, table, (((1,), (1,)), ((), ())), preferred_element_type=jnp.float32)

    return dot(high, table_hi) + (dot(low, table_hi) + dot(high, table_lo))


def times(high, low, table_hi, table_lo):
    dot = functools.partial(jnp.dot, preferred_element_type=jnp.float32)
    return dot(high, table_hi) + (dot(low, table_hi) + dot(high, table_lo))


def multiplied(left, right, conj, residue):
    a_re, a_im = left
    b_re, b_im = right
    rr, ii, ri, ir = a_re * b_re, a_im * b_im, a_re * b_im, a_im * b_re
    if conj:
        re, im = rr + ii, ri - ir
    else:
        re, im = rr - ii, ri + ir
    if residue == 0:
        shared = lax.broadcasted_iota(jnp.int32, re.shape, 1) == 0
        re, im = jnp.where(shared, 0.5 * rr, re), jnp.where(shared, 0.5 * ii, im)
    return re, im


def window_blocks(rate):
    rate = jnp.broadcast_to(rate, (rate.shape[0], LANES))
    place = lax.broadcasted_iota(jnp.int32, rate.shape, 1).astype(jnp.float32)
    first = jnp.sqrt(2.0 * rate) * jnp.exp(-rate * place) * (1.0 / (BLOCKS * LANES))
    return [first * jnp.exp(rate * (-float(LANES) * a)) if a else first for a in range(BLOCKS)]


def fetched(sources, places, sems):
    copies = [pltpu.make_async_copy(src, dst, sems.at[i]) for i, (src, dst) in enumerate(zip(sources, places))]
    for copy in copies:
        copy.start()
    return copies


def filter_kernel(proj, rate, features, angle, spectra, filters, fold_hi, fold_lo, table_hi, table_lo):
    rows = proj.shape[0]
    for a in range(BLOCKS):
        terms = features[a * LANES : (a + 1) * LANES]
        filters[a] = lax.dot_general(proj[...], terms, (((1,), (1,)), ((), ())), preferred_element_type=jnp.float32)

    @pl.loop(0, rows // STEP)
    def _(step):
        at = pl.ds(pl.multiple_of(step * STEP, STEP), STEP)
        window = window_blocks(rate[at, :])
        store_folded(fold_hi, fold_lo, at, [filters[a, at, :] * window[a] for a in range(BLOCKS)])

    for residue in range(BLOCKS):
        make_table(angle, residue, table_hi, table_lo)
        spectra[residue] = times(fold_hi[residue], fold_lo[residue], table_hi[residue], table_lo[residue])


def places():
    place = lax.axis_index("seq")
    return [place] + [place ^ peer for peer in PEERS]


def main_kernel(*refs):
    received, (rate, filt, angle, features), sent = refs[:BLOCKS], refs[BLOCKS : BLOCKS + 4], refs[BLOCKS + 4 : 2 * BLOCKS + 4]
    (
        moved, results, one_hi, one_lo, two_hi, two_lo, spec, spec2, back, weighted_hi, weighted_lo, table_hi, table_lo,
    ) = refs[2 * BLOCKS + 4 :]
    count = moved.shape[1] // SENT
    value, inner, product = (moved.at[:, i * count : (i + 1) * count] for i in range(SENT))
    grad_value, grad_inner, outer_coded = (results.at[:, i * count : (i + 1) * count] for i in range(3))
    for place, block in zip(places(), received):
        moved[place] = block[...]

    def forward(residue):
        return times(one_hi[residue], one_lo[residue], table_hi[residue], table_lo[residue])

    def inverse(residue, rows):
        return times_transposed(
            two_hi[residue, rows, :], two_lo[residue, rows, :], table_hi[residue], table_lo[residue])

    def chunk(step):
        return pl.ds(pl.multiple_of(step * STEP, STEP), STEP), pl.ds(pl.multiple_of(count + step * STEP, STEP), STEP)

    def pair(ref, residue, rows):
        return ref[residue, rows, :LANES], ref[residue, rows, LANES:]

    upper, lower = slice(0, count), slice(count, 2 * count)

    @pl.loop(0, count // STEP)
    def _(step):
        at, below = chunk(step)
        store_folded(one_hi, one_lo, at, [value[a, at, :].astype(jnp.float32) for a in range(BLOCKS)])
        store_folded(one_hi, one_lo, below, [fourth_root(product[a, at, :], PRODUCT_SCALE) for a in range(BLOCKS)])

    for residue in range(BLOCKS):
        make_table(angle, residue, table_hi, table_lo)
        spec[residue] = forward(residue)
        put(two_hi, two_lo, (residue, upper), multiplied(
            pair(filt, residue, upper), pair(spec, residue, upper), False, residue))
        put(two_hi, two_lo, (residue, lower), multiplied(
            pair(filt, residue, lower), pair(spec, residue, lower), True, residue))
        rows = slice(0, 2 * count)
        back[residue, rows, :] = inverse(residue, rows)

    @pl.loop(0, count // STEP)
    def _(step):
        at, below = chunk(step)
        gate = [inner[a, at, :].astype(jnp.float32) for a in range(BLOCKS)]
        inner_act = unfold([pair(back, residue, at) for residue in range(BLOCKS)])
        store_folded(one_hi, one_lo, at, [gate[a] * inner_act[a] for a in range(BLOCKS)])
        grad_mixed = unfold([pair(back, residue, below) for residue in range(BLOCKS)])
        for a in range(BLOCKS):
            grad_inner[a, at, :] = (grad_mixed[a] * inner_act[a]).astype(jnp.bfloat16)
        store_folded(one_hi, one_lo, below, [gate[a] * grad_mixed[a] for a in range(BLOCKS)])

    for residue in range(BLOCKS):
        spec2[...] = forward(residue)
        mixed = spec2[upper, :LANES], spec2[upper, LANES:]
        inner_grad = spec2[lower, :LANES], spec2[lower, LANES:]
        products = (
            multiplied(pair(filt, residue, lower), mixed, False, residue),
            multiplied(pair(filt, residue, upper), inner_grad, True, residue),
            multiplied(pair(spec, residue, upper), inner_grad, True, residue),
            multiplied(mixed, pair(spec, residue, lower), True, residue),
        )
        for place, product in enumerate(products):
            put(two_hi, two_lo, (residue, slice(place * count, (place + 1) * count)), product)
        back[residue] = inverse(residue, slice(0, 4 * count))

    @pl.loop(0, count // STEP)
    def _(step):
        def signal(place):
            at = pl.ds(pl.multiple_of(place * count + step * STEP, STEP), STEP)
            return unfold([pair(back, residue, at) for residue in range(BLOCKS)])

        at, below = chunk(step)
        outer_act = signal(0)
        for a in range(BLOCKS):
            outer_coded[a, at, :] = fourth_power(outer_act[a], OUTER_SCALE)
        value_grad = signal(1)
        for a in range(BLOCKS):
            grad_value[a, at, :] = value_grad[a].astype(jnp.bfloat16)
        for place, rows in ((2, at), (3, below)):
            filter_grad = signal(place)
            window = window_blocks(rate[rows, :])
            for a in range(BLOCKS):
                high, low = halves(filter_grad[a] * window[a])
                lanes = slice(a * LANES, (a + 1) * LANES)
                weighted_hi[rows, lanes] = high
                weighted_lo[rows, lanes] = low

    dot = functools.partial(jnp.dot, preferred_element_type=jnp.float32)
    total = (dot(weighted_hi[...], features[...]) + dot(weighted_lo[...], features[...])).T
    half = total.shape[0] // 2
    total = total[:half] + total[half:]
    for place in range(2):
        part = total[:, place * count : (place + 1) * count]
        coded = (part * jnp.abs(part)).astype(jnp.bfloat16)
        for a in range(BLOCKS):
            results[a, 3 * count + place * half : 3 * count + (place + 1) * half] = coded
    for place, block in zip(places(), sent):
        block[...] = results[place]


def device_call(kernel, out_shape, scratch, in_vmem, out_vmem, name, limit):
    def spec(inside):
        return pl.BlockSpec(memory_space=pltpu.VMEM if inside else pl.ANY)

    return pl.pallas_call(
        kernel,
        out_shape=out_shape,
        in_specs=[spec(inside) for inside in in_vmem],
        out_specs=[spec(inside) for inside in out_vmem],
        scratch_shapes=scratch,
        compiler_params=pltpu.CompilerParams(vmem_limit_bytes=limit * 2**20),
        name=name,
    )


def filter_spectra(proj_rows, rates, terms, angle):
    rows = proj_rows.shape[0]
    twice = jnp.concatenate([proj_rows, proj_rows], 1)
    bf, f32 = jnp.bfloat16, jnp.float32
    width = 2 * LANES
    return device_call(
        filter_kernel,
        [jax.ShapeDtypeStruct((BLOCKS, rows, width), f32)],
        [pltpu.VMEM((BLOCKS, rows, LANES), f32)]
        + [pltpu.VMEM((BLOCKS, rows, width), bf)] * 2
        + [pltpu.VMEM((BLOCKS, width, width), bf)] * 2,
        (True,) * 4,
        (True,),
        "filter_spectra",
        16,
    )(twice, rates.reshape(rows, 1), terms, angle)[0]


def operator_grads(received, rates, spectra, angle, terms):
    count = received[0].shape[0] // SENT
    bf, f32 = jnp.bfloat16, jnp.float32
    width = 2 * LANES
    return device_call(
        main_kernel,
        [jax.ShapeDtypeStruct((RETURNED * count, LANES), bf)] * BLOCKS,
        [pltpu.VMEM((BLOCKS, SENT * count, LANES), bf), pltpu.VMEM((BLOCKS, RETURNED * count, LANES), bf)]
        + [pltpu.VMEM((BLOCKS, 2 * count, width), bf)] * 2
        + [pltpu.VMEM((BLOCKS, 4 * count, width), bf)] * 2
        + [pltpu.VMEM((BLOCKS, 2 * count, width), f32), pltpu.VMEM((2 * count, width), f32),
           pltpu.VMEM((BLOCKS, 4 * count, width), f32)]
        + [pltpu.VMEM((2 * count, BLOCKS * LANES), bf)] * 2
        + [pltpu.VMEM((BLOCKS, width, width), bf)] * 2,
        (True,) * (BLOCKS + 4),
        (True,) * BLOCKS,
        "operator_grads",
        MAIN_LIMIT,
    )(*received, rates.reshape(2 * count, 1), spectra, angle, terms)


def pack_kernel(value, inner, outer, grad, *refs):
    sent, (outer_in, grad_in, sems) = refs[:BLOCKS], refs[BLOCKS:]
    count = sent[0].shape[0] // SENT
    first = fetched((outer, grad), (outer_in, grad_in), sems)
    rest = []
    for i, (place, block) in enumerate(zip(places(), sent)):
        for j, source in enumerate((value, inner)):
            copy = pltpu.make_async_copy(source.at[place], block.at[j * count : (j + 1) * count], sems.at[2 + 2 * i + j])
            copy.start()
            rest.append(copy)
    for copy in first:
        copy.wait()
    for place, block in zip(places(), sent):
        both = grad_in[place].astype(jnp.float32) * outer_in[place].astype(jnp.float32)
        block[2 * count :] = fourth_power(both, PRODUCT_SCALE)
    for copy in rest:
        copy.wait()


def packed(*arrays):
    channels, lanes = arrays[0].shape
    count = channels // BLOCKS
    held = pltpu.VMEM((BLOCKS, count, lanes), jnp.bfloat16)
    return device_call(
        pack_kernel,
        [jax.ShapeDtypeStruct((SENT * count, lanes), jnp.bfloat16)] * BLOCKS,
        [held, held, pltpu.SemaphoreType.DMA((2 + 2 * BLOCKS,))],
        (False,) * 4,
        (True,) * BLOCKS,
        "packed",
        PACK_LIMIT,
    )(*(x.reshape(BLOCKS, count, lanes) for x in arrays))


def exchanged(blocks):
    swaps = [[(i, i ^ peer) for i in range(BLOCKS)] for peer in PEERS]
    return [blocks[0]] + [lax.ppermute(block, "seq", swap) for block, swap in zip(blocks[1:], swaps)]


def sum_kernel(*refs):
    received, total = refs[:-1], refs[-1]
    first = 3 * (received[0].shape[0] // RETURNED)
    part = jnp.zeros(total.shape, jnp.float32)
    for block in received:
        size = jnp.abs(block[first:].astype(jnp.float32))
        part = part + jnp.sum(size.reshape((-1,) + total.shape), 0)
    total[...] = jnp.broadcast_to(jnp.sum(part, keepdims=True), total.shape)


def square_total(received):
    return device_call(
        sum_kernel, [jax.ShapeDtypeStruct((8, LANES), jnp.float32)], [], (True,) * BLOCKS, (True,), "square_total", 16
    )(*received)[0]


def unpack_kernel(*refs):
    received, (grad, *outs), (grad_in, outer_out, sems) = refs[:BLOCKS], refs[BLOCKS : BLOCKS + 4], refs[BLOCKS + 4 :]
    count = received[0].shape[0] // RETURNED
    fetch = pltpu.make_async_copy(grad, grad_in, sems.at[2 * BLOCKS])
    fetch.start()
    copies = []
    for i, (place, block) in enumerate(zip(places(), received)):
        for j, out in enumerate(outs[:2]):
            copy = pltpu.make_async_copy(block.at[j * count : (j + 1) * count], out.at[place], sems.at[2 * i + j])
            copy.start()
            copies.append(copy)
    fetch.wait()
    for place, block in zip(places(), received):
        act = fourth_root(block[2 * count : 3 * count], OUTER_SCALE)
        outer_out[place] = (grad_in[place].astype(jnp.float32) * act).astype(jnp.bfloat16)
    last = pltpu.make_async_copy(outer_out, outs[2], sems.at[2 * BLOCKS + 1])
    last.start()
    for copy in (*copies, last):
        copy.wait()


def unpacked(received, grad):
    channels, lanes = grad.shape
    count = channels // BLOCKS
    block = jax.ShapeDtypeStruct((BLOCKS, count, lanes), jnp.bfloat16)
    held = pltpu.VMEM(block.shape, block.dtype)
    grads = device_call(
        unpack_kernel,
        [block] * 3,
        [held, held, pltpu.SemaphoreType.DMA((2 * BLOCKS + 2,))],
        (True,) * BLOCKS + (False,),
        (False,) * 3,
        "unpacked",
        16,
    )(*received, grad.reshape(block.shape))
    return [x.reshape(channels, lanes) for x in grads]


def scale_kernel(entries, *refs):
    received, sums, (out, held, sem) = refs[:BLOCKS], refs[BLOCKS:-3], refs[-3:]
    count = received[0].shape[0] // RETURNED
    total = sums[0][...]
    for part in sums[1:]:
        total = total + part[...]
    scale = lax.rsqrt(total * (1.0 / entries) + 1e-06)[:1]
    features = held.shape[1]
    for place, block in zip(places(), received):
        lanes = pl.ds(pl.multiple_of(place * LANES, LANES), LANES)
        for i in range(2):
            first = 3 * count + i * features
            coded = block[first : first + features].astype(jnp.float32)
            size = jnp.sqrt(jnp.abs(coded)) * scale
            held[i, :, lanes] = jnp.where(coded < 0, -size, size)
    copy = pltpu.make_async_copy(held, out, sem)
    copy.start()
    copy.wait()


def scaled(received, sums, entries, features):
    shape = (2, features, BLOCKS * LANES)
    return device_call(
        functools.partial(scale_kernel, entries),
        [jax.ShapeDtypeStruct(shape, jnp.float32)],
        [pltpu.VMEM(shape, jnp.float32), pltpu.SemaphoreType.DMA],
        (True,) * (BLOCKS + len(sums)),
        (False,),
        "scaled",
        16,
    )(*received, *sums)[0]


highest = lax.Precision.HIGHEST


def angle_table(rows, cols, period):
    row_idx = lax.broadcasted_iota(jnp.int32, (rows, cols), 0)
    col_idx = lax.broadcasted_iota(jnp.int32, (rows, cols), 1)
    angle = (row_idx * col_idx % period).astype(jnp.float32) * (2.0 * math.pi / period)
    return (jnp.cos(angle), jnp.sin(angle))


def split_length(total):
    return max((factor for factor in range(2, math.isqrt(total) + 1, 2) if total % factor == 0))


def forward_dft(signal):
    rows, length = signal.shape
    total = 2 * length
    first = split_length(total)
    second = total // first
    half = first // 2
    shaped = signal.reshape(rows, half, second)
    cos_one, sin_one = angle_table(half, first, first)
    part_re = jnp.einsum("mab,ak->mkb", shaped, cos_one, precision=highest)
    part_im = -jnp.einsum("mab,ak->mkb", shaped, sin_one, precision=highest)
    twist_cos, twist_sin = angle_table(first, second, total)
    turned_re = part_re * twist_cos + part_im * twist_sin
    turned_im = part_im * twist_cos - part_re * twist_sin
    cos_two, sin_two = angle_table(second, second, second)
    out_re = jnp.einsum("mkb,bl->mkl", turned_re, cos_two, precision=highest) + jnp.einsum(
        "mkb,bl->mkl", turned_im, sin_two, precision=highest
    )
    out_im = jnp.einsum("mkb,bl->mkl", turned_im, cos_two, precision=highest) - jnp.einsum(
        "mkb,bl->mkl", turned_re, sin_two, precision=highest
    )
    return (out_re, out_im)


def inverse_dft(spectrum):
    spec_re, spec_im = spectrum
    rows, first, second = spec_re.shape
    total = first * second
    half = first // 2
    cos_two, sin_two = angle_table(second, second, second)
    part_re = jnp.einsum("mkl,lb->mkb", spec_re, cos_two, precision=highest) - jnp.einsum(
        "mkl,lb->mkb", spec_im, sin_two, precision=highest
    )
    part_im = jnp.einsum("mkl,lb->mkb", spec_re, sin_two, precision=highest) + jnp.einsum(
        "mkl,lb->mkb", spec_im, cos_two, precision=highest
    )
    twist_cos, twist_sin = angle_table(first, second, total)
    turned_re = part_re * twist_cos - part_im * twist_sin
    turned_im = part_re * twist_sin + part_im * twist_cos
    cos_one, sin_one = angle_table(half, first, first)
    result = jnp.einsum("mkb,ak->mab", turned_re, cos_one, precision=highest) - jnp.einsum(
        "mkb,ak->mab", turned_im, sin_one, precision=highest
    )
    return result.reshape(rows, half * second) / total


def product_of(left, right, conj_left):
    left_re, left_im = left
    right_re, right_im = right
    if conj_left:
        left_im = -left_im
    return (left_re * right_re - left_im * right_im, left_re * right_im + left_im * right_re)


def rows_of(spectrum, start, count):
    return (spectrum[0][start : start + count], spectrum[1][start : start + count])


def joined(upper, lower):
    return (jnp.concatenate([upper[0], lower[0]], 0), jnp.concatenate([upper[1], lower[1]], 0))


def general_body(value_in, gate_inner, gate_outer, out_grad, filter_proj, decay, frequency):
    seq_pos = lax.axis_index("seq")
    value_cols, inner_cols, outer_cols, grad_cols = (
        lax.all_to_all(value_in, "seq", split_axis=0, concat_axis=1, tiled=True),
        lax.all_to_all(gate_inner, "seq", split_axis=0, concat_axis=1, tiled=True),
        lax.all_to_all(gate_outer, "seq", split_axis=0, concat_axis=1, tiled=True),
        lax.all_to_all(out_grad, "seq", split_axis=0, concat_axis=1, tiled=True),
    )
    count = value_cols.shape[0]
    length = value_cols.shape[1]
    first_row = seq_pos * count
    proj_rows = lax.dynamic_slice_in_dim(filter_proj, first_row, count, 1).astype(jnp.float32)
    rates = lax.dynamic_slice_in_dim(decay, first_row, count, 1)
    positions = lax.iota(jnp.float32, length)
    features = jnp.sin(frequency[None, :] * (positions[:, None] + 1.0))
    window = jnp.sqrt(2.0 * rates)[:, :, None] * jnp.exp(-rates[:, :, None] * positions)
    filters = jnp.einsum("kcf,tf->kct", proj_rows, features, precision=highest) * window
    value_f = value_cols.astype(jnp.float32)
    inner_f = inner_cols.astype(jnp.float32)
    spectra = forward_dft(jnp.concatenate([filters[0], filters[1], value_f], 0))
    inner_spec = rows_of(spectra, 0, count)
    outer_spec = rows_of(spectra, count, count)
    value_spec = rows_of(spectra, 2 * count, count)
    inner_act = inverse_dft(product_of(inner_spec, value_spec, False))
    mixed = inner_f * inner_act
    mixed_spec = forward_dft(mixed)
    outer_act = inverse_dft(product_of(outer_spec, mixed_spec, False))
    outer_f = outer_cols.astype(jnp.float32)
    grad_f = grad_cols.astype(jnp.float32)
    grad_outer = grad_f * outer_act
    grad_spec = forward_dft(grad_f * outer_f)
    outer_back = inverse_dft(
        joined(product_of(outer_spec, grad_spec, True), product_of(mixed_spec, grad_spec, True))
    )
    grad_mixed = outer_back[:count]
    grad_outer_filter = outer_back[count:]
    grad_inner = grad_mixed * inner_act
    inner_grad_spec = forward_dft(grad_mixed * inner_f)
    inner_back = inverse_dft(
        joined(
            product_of(inner_spec, inner_grad_spec, True),
            product_of(value_spec, inner_grad_spec, True),
        )
    )
    grad_value = inner_back[:count]
    grad_inner_filter = inner_back[count:]
    value_out, inner_out, outer_out = (
        lax.all_to_all(
            grad_value.astype(jnp.bfloat16), "seq", split_axis=1, concat_axis=0, tiled=True
        ),
        lax.all_to_all(
            grad_inner.astype(jnp.bfloat16), "seq", split_axis=1, concat_axis=0, tiled=True
        ),
        lax.all_to_all(
            grad_outer.astype(jnp.bfloat16), "seq", split_axis=1, concat_axis=0, tiled=True
        ),
    )
    weighted = jnp.stack([grad_inner_filter, grad_outer_filter]) * window
    own_grad = jnp.einsum("kct,tf->kcf", weighted, features, precision=highest)
    proj_grad = lax.all_gather(own_grad, "seq", axis=1, tiled=True)
    square_sum = lax.psum(jnp.sum(proj_grad * proj_grad), "ch")
    entries = proj_grad.size * lax.axis_size("ch")
    scale = lax.rsqrt(square_sum / entries + 1e-06)
    return (value_out, inner_out, outer_out, proj_grad * scale)


def body(value_in, gate_inner, gate_outer, out_grad, filter_proj, decay, frequency):
    seq_pos = lax.axis_index("seq")
    channels, lanes = value_in.shape
    count = channels // BLOCKS
    length = BLOCKS * lanes
    angle = jnp.asarray(angles())

    def own_rows(x):
        rows = lax.dynamic_slice_in_dim(x, seq_pos * count, count, 1)
        return rows.reshape((2 * count,) + x.shape[2:])

    received = exchanged(packed(value_in, gate_inner, gate_outer, out_grad))
    rates = own_rows(decay)
    features = jnp.sin(frequency[None, :] * (lax.iota(jnp.float32, length)[:, None] + 1.0))
    terms = jnp.concatenate(split_features(features), 1)
    spectra = filter_spectra(own_rows(filter_proj), rates, terms, angle)
    back = exchanged(operator_grads(received, rates, spectra, angle, terms))
    own_sum = square_total(back)
    groups = lax.axis_size("ch")
    sums = [own_sum] + [
        lax.ppermute(own_sum, "ch", [(i, i ^ hop) for i in range(groups)]) for hop in range(1, groups)
    ]
    grads = unpacked(back, out_grad)
    proj_grad = scaled(back, sums, filter_proj.size * groups, features.shape[1])
    return (*grads, proj_grad.transpose(0, 2, 1))


def solution(mesh):
    def chosen(*arrays):
        whole = arrays[0].shape[1] == LANES and arrays[0].shape[0] % (BLOCKS * STEP) == 0
        fits = lax.axis_size("seq") == BLOCKS and lax.axis_size("ch") == 4
        return body(*arrays) if whole and fits else general_body(*arrays)

    split = P("ch", "seq")
    rows = P(None, "ch", None)
    return jax.shard_map(
        chosen,
        mesh=mesh,
        in_specs=(split, split, split, split, rows, P(None, "ch"), P()),
        out_specs=(split, split, split, rows),
        check_vma=False,
    )
```

```python
import math
import functools
import numpy as np
import ml_dtypes
import jax
import jax.numpy as jnp
from jax import lax
from jax.experimental import pallas as pl
from jax.experimental.pallas import tpu as pltpu
from jax.sharding import PartitionSpec as P

BLOCKS = 8
LANES = 128
COS1, COS2, COS3 = (math.cos(math.pi / 8), math.cos(math.pi / 4), math.cos(3 * math.pi / 8))
STEP = 16
SIN_AT, SIGN_AT = 16, 32
FIRST_PEERS = (1, 4, 2, 6, 3, 5, 7)
LAST_PEERS = (1, 4, 6, 2, 5, 7, 3)
HELD_FOR = (1,)
NEAR = 1
SENT, RETURNED = 3, 4
PACK_LIMIT, MAIN_LIMIT = 60, 32
PRODUCT_SCALE, OUTER_SCALE = 2.0**24, 2.0**-3


def angles():
    lane = np.arange(LANES)
    whole = 2 * np.pi * np.outer(lane, lane) / LANES
    turn = 2 * np.pi * np.outer(lane, np.arange(BLOCKS + 1)) / (2 * BLOCKS * LANES)
    turn[:, BLOCKS] += np.pi * lane
    columns = np.zeros((LANES, LANES))
    columns[:, : BLOCKS + 1] = np.cos(turn)
    columns[:, SIN_AT : SIN_AT + BLOCKS + 1] = np.sin(turn)
    columns[:, SIGN_AT] = 1.0 - 2.0 * (lane % 2)
    return np.stack([np.cos(whole), np.sin(whole), columns]).astype(np.float32)


def fold(x):
    s = [x[a] + x[a + 4] for a in range(4)]
    d = [x[a] - x[a + 4] for a in range(4)]
    t0, t1 = s[0] + s[2], s[1] + s[3]
    u0, u1 = s[0] - s[2], s[1] - s[3]
    p, w = (d[1] - d[3]) * COS2, (d[1] + d[3]) * COS2
    p1, p2, p3 = x[1] - x[7], (x[2] - x[6]) * COS2, x[3] - x[5]
    n1, n2, n3 = x[1] + x[7], (x[2] + x[6]) * COS2, x[3] + x[5]
    a0, b0 = x[0] + p2, x[0] - p2
    c0, d0 = p1 * COS1 + p3 * COS3, p1 * COS3 - p3 * COS1
    a1, b1 = n2 + x[4], n2 - x[4]
    c1, d1 = n1 * COS3 + n3 * COS1, n1 * COS1 - n3 * COS3
    return (
        (t0 + t1, t0 - t1),
        (a0 + c0, c1 + a1),
        (d[0] + p, d[2] + w),
        (b0 + d0, d1 + b1),
        (u0, u1),
        (b0 - d0, d1 - b1),
        (d[0] - p, w - d[2]),
        (a0 - c0, c1 - a1),
    )


def unfold(z):
    (z0, z8), (r1, i1), (r2, i2), (r3, i3), (r4, i4), (r5, i5), (r6, i6), (r7, i7) = z
    even, odd = z0 + z8, z0 - z8
    g = [even + r4, odd + i4, even - r4, odd - i4]
    dr, di = r2 - r6, i2 + i6
    h = [r2 + r6, (dr + di) * COS2, i2 - i6, (di - dr) * COS2]
    rs, rd, ts, td = r1 + r7, r1 - r7, r3 + r5, r3 - r5
    js, jd, ks, kd = i1 + i7, i1 - i7, i3 + i5, i3 - i5
    k = [None, rd * COS1 + td * COS3, (rs - ts) * COS2, rd * COS3 - td * COS1]
    m = [None, js * COS3 + ks * COS1, (jd + kd) * COS2, js * COS1 - ks * COS3]
    o = [rs + ts, k[1] + m[1], k[2] + m[2], k[3] + m[3], jd - kd, m[3] - k[3], m[2] - k[2], m[1] - k[1]]
    return [g[a] + h[a] + o[a] for a in range(4)] + [g[a] - h[a] + o[a + 4] for a in range(4)]


def fourth_power(x, scale):
    x = x * scale
    return (x * x * (x * jnp.abs(x))).astype(jnp.bfloat16)


def fourth_root(code, scale):
    code = code.astype(jnp.float32)
    size = jnp.sqrt(jnp.sqrt(jnp.abs(code))) * (1.0 / scale)
    return jnp.where(code < 0, -size, size)


def halves(x):
    high = x.astype(jnp.bfloat16)
    return high, (x - high.astype(jnp.float32)).astype(jnp.bfloat16)


def split_features(features):
    high = lax.reduce_precision(features, 8, 7)
    return high.astype(jnp.bfloat16), (features - high).astype(jnp.bfloat16)


def put(hi_ref, lo_ref, index, parts):
    for part, x in enumerate(parts):
        high, low = halves(x)
        lanes = slice(part * LANES, (part + 1) * LANES)
        hi_ref[index + (lanes,)] = high
        lo_ref[index + (lanes,)] = low


def store_folded(hi_ref, lo_ref, rows, blocks):
    for residue, parts in enumerate(fold(blocks)):
        put(hi_ref, lo_ref, (residue, rows), parts)


def make_table(angle, residue, table_hi, table_lo):
    def turned(column):
        cos, sin = angle[0], angle[1]
        turn_cos, turn_sin = angle[2, :, column : column + 1], angle[2, :, SIN_AT + column : SIN_AT + column + 1]
        return cos * turn_cos - sin * turn_sin, -(sin * turn_cos + cos * turn_sin)

    real, imag = turned(residue)
    if residue:
        blocks = ((real, imag), (imag, -real))
    else:
        lane = lax.broadcasted_iota(jnp.int32, real.shape, 1)
        below = lane < LANES // 2
        sign = jnp.broadcast_to(angle[2, :, SIGN_AT : SIGN_AT + 1], real.shape)
        top = jnp.where(below, real, 0.0), jnp.where(lane == 0, sign, jnp.where(below, imag, 0.0))
        blocks = (top, tuple(jnp.where(below, 0.0, x) for x in turned(BLOCKS)))
    for i, row in enumerate(blocks):
        for j, x in enumerate(row):
            high, low = halves(x)
            at = residue, slice(i * LANES, (i + 1) * LANES), slice(j * LANES, (j + 1) * LANES)
            table_hi[at] = high
            table_lo[at] = low


def times_transposed(high, low, table_hi, table_lo):
    def dot(x, table):
        return lax.dot_general(x, table, (((1,), (1,)), ((), ())), preferred_element_type=jnp.float32)

    return dot(high, table_hi) + (dot(low, table_hi) + dot(high, table_lo))


def times(high, low, table_hi, table_lo):
    dot = functools.partial(jnp.dot, preferred_element_type=jnp.float32)
    return dot(high, table_hi) + (dot(low, table_hi) + dot(high, table_lo))


def multiplied(left, right, conj, residue):
    a_re, a_im = left
    b_re, b_im = right
    rr, ii, ri, ir = a_re * b_re, a_im * b_im, a_re * b_im, a_im * b_re
    if conj:
        re, im = rr + ii, ri - ir
    else:
        re, im = rr - ii, ri + ir
    if residue == 0:
        shared = lax.broadcasted_iota(jnp.int32, re.shape, 1) == 0
        re, im = jnp.where(shared, 0.5 * rr, re), jnp.where(shared, 0.5 * ii, im)
    return re, im


def window_blocks(rate):
    rate = jnp.broadcast_to(rate, (rate.shape[0], LANES))
    place = lax.broadcasted_iota(jnp.int32, rate.shape, 1).astype(jnp.float32)
    first = jnp.sqrt(2.0 * rate) * jnp.exp(-rate * place) * (1.0 / (BLOCKS * LANES))
    return [first * jnp.exp(rate * (-float(LANES) * a)) if a else first for a in range(BLOCKS)]


def fetched(sources, places, sems):
    copies = [pltpu.make_async_copy(src, dst, sems.at[i]) for i, (src, dst) in enumerate(zip(sources, places))]
    for copy in copies:
        copy.start()
    return copies


def filter_kernel(proj, rate, features, angle, spectra, filters, fold_hi, fold_lo, table_hi, table_lo):
    rows = proj.shape[0]
    for a in range(BLOCKS):
        terms = features[a * LANES : (a + 1) * LANES]
        filters[a] = lax.dot_general(proj[...], terms, (((1,), (1,)), ((), ())), preferred_element_type=jnp.float32)

    @pl.loop(0, rows // STEP)
    def _(step):
        at = pl.ds(pl.multiple_of(step * STEP, STEP), STEP)
        window = window_blocks(rate[at, :])
        store_folded(fold_hi, fold_lo, at, [filters[a, at, :] * window[a] for a in range(BLOCKS)])

    for residue in range(BLOCKS):
        make_table(angle, residue, table_hi, table_lo)
        spectra[residue] = times(fold_hi[residue], fold_lo[residue], table_hi[residue], table_lo[residue])


def direct(peer):
    return not peer & NEAR


def places(peers):
    place = lax.axis_index("seq")
    return [place] + [place ^ peer for peer in peers]


def main_kernel(*refs):
    received, (rate, filt, angle, features), sent = refs[:BLOCKS], refs[BLOCKS : BLOCKS + 4], refs[BLOCKS + 4 : 2 * BLOCKS + 4]
    (
        moved, results, one_hi, one_lo, two_hi, two_lo, spec, spec2, back, weighted_hi, weighted_lo, table_hi, table_lo,
    ) = refs[2 * BLOCKS + 4 :]
    count = moved.shape[1] // SENT
    value, inner, product = (moved.at[:, i * count : (i + 1) * count] for i in range(SENT))
    grad_value, grad_inner, outer_coded = (results.at[:, i * count : (i + 1) * count] for i in range(3))
    for place, block in zip(places(FIRST_PEERS), received):
        moved[place] = block[...]

    def forward(residue):
        return times(one_hi[residue], one_lo[residue], table_hi[residue], table_lo[residue])

    def inverse(residue, rows):
        return times_transposed(
            two_hi[residue, rows, :], two_lo[residue, rows, :], table_hi[residue], table_lo[residue])

    def chunk(step):
        return pl.ds(pl.multiple_of(step * STEP, STEP), STEP), pl.ds(pl.multiple_of(count + step * STEP, STEP), STEP)

    def pair(ref, residue, rows):
        return ref[residue, rows, :LANES], ref[residue, rows, LANES:]

    upper, lower = slice(0, count), slice(count, 2 * count)

    @pl.loop(0, count // STEP, unroll=count // STEP)
    def _(step):
        at, below = chunk(step)
        store_folded(one_hi, one_lo, at, [value[a, at, :].astype(jnp.float32) for a in range(BLOCKS)])
        store_folded(one_hi, one_lo, below, [fourth_root(product[a, at, :], PRODUCT_SCALE) for a in range(BLOCKS)])

    for residue in range(BLOCKS):
        make_table(angle, residue, table_hi, table_lo)
        spec[residue] = forward(residue)
        put(two_hi, two_lo, (residue, upper), multiplied(
            pair(filt, residue, upper), pair(spec, residue, upper), False, residue))
        put(two_hi, two_lo, (residue, lower), multiplied(
            pair(filt, residue, lower), pair(spec, residue, lower), True, residue))
        rows = slice(0, 2 * count)
        back[residue, rows, :] = inverse(residue, rows)

    @pl.loop(0, count // STEP, unroll=count // STEP)
    def _(step):
        at, below = chunk(step)
        gate = [inner[a, at, :].astype(jnp.float32) for a in range(BLOCKS)]
        inner_act = unfold([pair(back, residue, at) for residue in range(BLOCKS)])
        store_folded(one_hi, one_lo, at, [gate[a] * inner_act[a] for a in range(BLOCKS)])
        grad_mixed = unfold([pair(back, residue, below) for residue in range(BLOCKS)])
        for a in range(BLOCKS):
            grad_inner[a, at, :] = (grad_mixed[a] * inner_act[a]).astype(jnp.bfloat16)
        store_folded(one_hi, one_lo, below, [gate[a] * grad_mixed[a] for a in range(BLOCKS)])

    for residue in range(BLOCKS):
        spec2[...] = forward(residue)
        mixed = spec2[upper, :LANES], spec2[upper, LANES:]
        inner_grad = spec2[lower, :LANES], spec2[lower, LANES:]
        products = (
            multiplied(pair(filt, residue, lower), mixed, False, residue),
            multiplied(pair(filt, residue, upper), inner_grad, True, residue),
            multiplied(pair(spec, residue, upper), inner_grad, True, residue),
            multiplied(mixed, pair(spec, residue, lower), True, residue),
        )
        for place, product in enumerate(products):
            put(two_hi, two_lo, (residue, slice(place * count, (place + 1) * count)), product)
        back[residue] = inverse(residue, slice(0, 4 * count))

    @pl.loop(0, count // STEP, unroll=count // STEP)
    def _(step):
        def signal(place):
            at = pl.ds(pl.multiple_of(place * count + step * STEP, STEP), STEP)
            return unfold([pair(back, residue, at) for residue in range(BLOCKS)])

        at, below = chunk(step)
        outer_act = signal(0)
        for a in range(BLOCKS):
            outer_coded[a, at, :] = fourth_power(outer_act[a], OUTER_SCALE)
        value_grad = signal(1)
        for a in range(BLOCKS):
            grad_value[a, at, :] = value_grad[a].astype(jnp.bfloat16)
        for place, rows in ((2, at), (3, below)):
            filter_grad = signal(place)
            window = window_blocks(rate[rows, :])
            for a in range(BLOCKS):
                high, low = halves(filter_grad[a] * window[a])
                lanes = slice(a * LANES, (a + 1) * LANES)
                weighted_hi[rows, lanes] = high
                weighted_lo[rows, lanes] = low

    dot = functools.partial(jnp.dot, preferred_element_type=jnp.float32)
    total = (dot(weighted_hi[...], features[...]) + dot(weighted_lo[...], features[...])).T
    half = total.shape[0] // 2
    total = total[:half] + total[half:]
    for place in range(2):
        part = total[:, place * count : (place + 1) * count]
        coded = (part * jnp.abs(part)).astype(jnp.bfloat16)
        for a in range(BLOCKS):
            results[a, 3 * count + place * half : 3 * count + (place + 1) * half] = coded
    for place, block in zip(places(LAST_PEERS), sent):
        block[...] = results[place, : block.shape[0]]


def device_call(kernel, out_shape, scratch, in_vmem, out_vmem, name, limit):
    def spec(inside):
        return pl.BlockSpec(memory_space=pltpu.VMEM if inside else pl.ANY)

    return pl.pallas_call(
        kernel,
        out_shape=out_shape,
        in_specs=[spec(inside) for inside in in_vmem],
        out_specs=[spec(inside) for inside in out_vmem],
        scratch_shapes=scratch,
        compiler_params=pltpu.CompilerParams(vmem_limit_bytes=limit * 2**20),
        name=name,
    )


def filter_spectra(proj_rows, rates, terms, angle):
    rows = proj_rows.shape[0]
    twice = jnp.concatenate([proj_rows, proj_rows], 1)
    bf, f32 = jnp.bfloat16, jnp.float32
    width = 2 * LANES
    return device_call(
        filter_kernel,
        [jax.ShapeDtypeStruct((BLOCKS, rows, width), f32)],
        [pltpu.VMEM((BLOCKS, rows, LANES), f32)]
        + [pltpu.VMEM((BLOCKS, rows, width), bf)] * 2
        + [pltpu.VMEM((BLOCKS, width, width), bf)] * 2,
        (True,) * 4,
        (True,),
        "filter_spectra",
        16,
    )(twice, rates.reshape(rows, 1), terms, angle)[0]


def operator_grads(received, rates, spectra, angle, terms):
    count = received[0].shape[0] // SENT
    bf, f32 = jnp.bfloat16, jnp.float32
    width = 2 * LANES
    return device_call(
        main_kernel,
        [jax.ShapeDtypeStruct(((3 + direct(peer)) * count, LANES), bf) for peer in (0,) + LAST_PEERS],
        [pltpu.VMEM((BLOCKS, SENT * count, LANES), bf), pltpu.VMEM((BLOCKS, RETURNED * count, LANES), bf)]
        + [pltpu.VMEM((BLOCKS, 2 * count, width), bf)] * 2
        + [pltpu.VMEM((BLOCKS, 4 * count, width), bf)] * 2
        + [pltpu.VMEM((BLOCKS, 2 * count, width), f32), pltpu.VMEM((2 * count, width), f32),
           pltpu.VMEM((BLOCKS, 4 * count, width), f32)]
        + [pltpu.VMEM((2 * count, BLOCKS * LANES), bf)] * 2
        + [pltpu.VMEM((BLOCKS, width, width), bf)] * 2,
        (True,) * (BLOCKS + 4),
        (True,) * BLOCKS,
        "operator_grads",
        MAIN_LIMIT,
    )(*received, rates.reshape(2 * count, 1), spectra, angle, terms)


def pack_kernel(value, inner, outer, grad, *refs):
    sent, (outer_in, grad_in, sems) = refs[:BLOCKS], refs[BLOCKS:]
    count = sent[0].shape[0] // SENT
    first = fetched((outer, grad), (outer_in, grad_in), sems)
    rest = []
    for i, (place, block) in enumerate(zip(places(FIRST_PEERS), sent)):
        for j, source in enumerate((value, inner)):
            copy = pltpu.make_async_copy(source.at[place], block.at[j * count : (j + 1) * count], sems.at[2 + 2 * i + j])
            copy.start()
            rest.append(copy)
    for copy in first:
        copy.wait()
    for place, block in zip(places(FIRST_PEERS), sent):
        both = grad_in[place].astype(jnp.float32) * outer_in[place].astype(jnp.float32)
        block[2 * count :] = fourth_power(both, PRODUCT_SCALE)
    for copy in rest:
        copy.wait()


def packed(*arrays):
    channels, lanes = arrays[0].shape
    count = channels // BLOCKS
    held = pltpu.VMEM((BLOCKS, count, lanes), jnp.bfloat16)
    return device_call(
        pack_kernel,
        [jax.ShapeDtypeStruct((SENT * count, lanes), jnp.bfloat16)] * BLOCKS,
        [held, held, pltpu.SemaphoreType.DMA((2 + 2 * BLOCKS,))],
        (False,) * 4,
        (True,) * BLOCKS,
        "packed",
        PACK_LIMIT,
    )(*(x.reshape(BLOCKS, count, lanes) for x in arrays))


def exchanged(blocks, peers):
    swaps = [[(i, i ^ peer) for i in range(BLOCKS)] for peer in peers]
    return [blocks[0]] + [lax.ppermute(block, "seq", swap) for block, swap in zip(blocks[1:], swaps)]


def gather_kernel(*refs):
    received, out = refs[:-1], refs[-1]
    count = out.shape[0] // len(received)
    for i, block in enumerate(received):
        out[i * count : (i + 1) * count] = block[3 * count :]


def second_hop(blocks):
    count = blocks[0].shape[0] // RETURNED
    gathered = device_call(
        gather_kernel,
        [jax.ShapeDtypeStruct((len(blocks) * count, LANES), jnp.bfloat16)],
        [],
        (True,) * len(blocks),
        (True,),
        "gather_proj",
        16,
    )(*blocks)[0]
    return lax.ppermute(gathered, "seq", [(i, i ^ NEAR) for i in range(BLOCKS)])


def proj_parts(direct_blocks, relayed):
    peers = [0] + [peer for peer in LAST_PEERS if direct(peer)]
    count = relayed.shape[0] // len(peers)
    for peer, block in zip(peers, direct_blocks):
        yield peer, block[3 * count :].astype(jnp.float32)
    for i, peer in enumerate(peers):
        yield peer ^ NEAR, relayed[i * count : (i + 1) * count].astype(jnp.float32)


def sum_kernel(*refs):
    *blocks, relayed, total = refs
    part = jnp.zeros(total.shape, jnp.float32)
    for _, coded in proj_parts(blocks, relayed):
        part = part + jnp.sum(jnp.abs(coded).reshape((-1,) + total.shape), 0)
    total[...] = jnp.broadcast_to(jnp.sum(part, keepdims=True), total.shape)


def square_total(blocks, relayed):
    return device_call(
        sum_kernel,
        [jax.ShapeDtypeStruct((8, LANES), jnp.float32)],
        [],
        (True,) * (len(blocks) + 1),
        (True,),
        "square_total",
        16,
    )(*blocks, relayed)[0]


def unpack_kernel(*refs):
    received, (grad, *outs), (grad_in, outer_out, sems) = refs[:BLOCKS], refs[BLOCKS : BLOCKS + 4], refs[BLOCKS + 4 :]
    count = grad.shape[1]
    fetch = pltpu.make_async_copy(grad, grad_in, sems.at[2 * BLOCKS])
    fetch.start()
    copies = []
    for i, (place, block) in enumerate(zip(places(LAST_PEERS), received)):
        for j, out in enumerate(outs[:2]):
            copy = pltpu.make_async_copy(block.at[j * count : (j + 1) * count], out.at[place], sems.at[2 * i + j])
            copy.start()
            copies.append(copy)
    fetch.wait()
    for place, block in zip(places(LAST_PEERS), received):
        act = fourth_root(block[2 * count : 3 * count], OUTER_SCALE)
        outer_out[place] = (grad_in[place].astype(jnp.float32) * act).astype(jnp.bfloat16)
    last = pltpu.make_async_copy(outer_out, outs[2], sems.at[2 * BLOCKS + 1])
    last.start()
    for copy in (*copies, last):
        copy.wait()


def unpacked(received, grad):
    channels, lanes = grad.shape
    count = channels // BLOCKS
    block = jax.ShapeDtypeStruct((BLOCKS, count, lanes), jnp.bfloat16)
    held = pltpu.VMEM(block.shape, block.dtype)
    grads = device_call(
        unpack_kernel,
        [block] * 3,
        [held, held, pltpu.SemaphoreType.DMA((2 * BLOCKS + 2,))],
        (True,) * BLOCKS + (False,),
        (False,) * 3,
        "unpacked",
        16,
    )(*received, grad.reshape(block.shape))
    return [x.reshape(channels, lanes) for x in grads]


def scale_kernel(entries, blocks, *refs):
    received, relayed, sums, (out, held, sem) = refs[:blocks], refs[blocks], refs[blocks + 1 : -3], refs[-3:]
    total = sums[0][...]
    for part in sums[1:]:
        total = total + part[...]
    scale = lax.rsqrt(total * (1.0 / entries) + 1e-06)[:1]
    features = held.shape[1]
    own = lax.axis_index("seq")
    for peer, coded in proj_parts(received, relayed):
        lanes = pl.ds(pl.multiple_of((own ^ peer) * LANES, LANES), LANES)
        size = jnp.sqrt(jnp.abs(coded)) * scale
        both = jnp.where(coded < 0, -size, size)
        for i in range(2):
            held[i, :, lanes] = both[i * features : (i + 1) * features]
    copy = pltpu.make_async_copy(held, out, sem)
    copy.start()
    copy.wait()


def scaled(blocks, relayed, sums, entries, features):
    shape = (2, features, BLOCKS * LANES)
    return device_call(
        functools.partial(scale_kernel, entries, len(blocks)),
        [jax.ShapeDtypeStruct(shape, jnp.float32)],
        [pltpu.VMEM(shape, jnp.float32), pltpu.SemaphoreType.DMA],
        (True,) * (len(blocks) + 1 + len(sums)),
        (False,),
        "scaled",
        16,
    )(*blocks, relayed, *sums)[0]


highest = lax.Precision.HIGHEST


def angle_table(rows, cols, period):
    row_idx = lax.broadcasted_iota(jnp.int32, (rows, cols), 0)
    col_idx = lax.broadcasted_iota(jnp.int32, (rows, cols), 1)
    angle = (row_idx * col_idx % period).astype(jnp.float32) * (2.0 * math.pi / period)
    return (jnp.cos(angle), jnp.sin(angle))


def split_length(total):
    return max((factor for factor in range(2, math.isqrt(total) + 1, 2) if total % factor == 0))


def forward_dft(signal):
    rows, length = signal.shape
    total = 2 * length
    first = split_length(total)
    second = total // first
    half = first // 2
    shaped = signal.reshape(rows, half, second)
    cos_one, sin_one = angle_table(half, first, first)
    part_re = jnp.einsum("mab,ak->mkb", shaped, cos_one, precision=highest)
    part_im = -jnp.einsum("mab,ak->mkb", shaped, sin_one, precision=highest)
    twist_cos, twist_sin = angle_table(first, second, total)
    turned_re = part_re * twist_cos + part_im * twist_sin
    turned_im = part_im * twist_cos - part_re * twist_sin
    cos_two, sin_two = angle_table(second, second, second)
    out_re = jnp.einsum("mkb,bl->mkl", turned_re, cos_two, precision=highest) + jnp.einsum(
        "mkb,bl->mkl", turned_im, sin_two, precision=highest
    )
    out_im = jnp.einsum("mkb,bl->mkl", turned_im, cos_two, precision=highest) - jnp.einsum(
        "mkb,bl->mkl", turned_re, sin_two, precision=highest
    )
    return (out_re, out_im)


def inverse_dft(spectrum):
    spec_re, spec_im = spectrum
    rows, first, second = spec_re.shape
    total = first * second
    half = first // 2
    cos_two, sin_two = angle_table(second, second, second)
    part_re = jnp.einsum("mkl,lb->mkb", spec_re, cos_two, precision=highest) - jnp.einsum(
        "mkl,lb->mkb", spec_im, sin_two, precision=highest
    )
    part_im = jnp.einsum("mkl,lb->mkb", spec_re, sin_two, precision=highest) + jnp.einsum(
        "mkl,lb->mkb", spec_im, cos_two, precision=highest
    )
    twist_cos, twist_sin = angle_table(first, second, total)
    turned_re = part_re * twist_cos - part_im * twist_sin
    turned_im = part_re * twist_sin + part_im * twist_cos
    cos_one, sin_one = angle_table(half, first, first)
    result = jnp.einsum("mkb,ak->mab", turned_re, cos_one, precision=highest) - jnp.einsum(
        "mkb,ak->mab", turned_im, sin_one, precision=highest
    )
    return result.reshape(rows, half * second) / total


def product_of(left, right, conj_left):
    left_re, left_im = left
    right_re, right_im = right
    if conj_left:
        left_im = -left_im
    return (left_re * right_re - left_im * right_im, left_re * right_im + left_im * right_re)


def rows_of(spectrum, start, count):
    return (spectrum[0][start : start + count], spectrum[1][start : start + count])


def joined(upper, lower):
    return (jnp.concatenate([upper[0], lower[0]], 0), jnp.concatenate([upper[1], lower[1]], 0))


def general_body(value_in, gate_inner, gate_outer, out_grad, filter_proj, decay, frequency):
    seq_pos = lax.axis_index("seq")
    value_cols, inner_cols, outer_cols, grad_cols = (
        lax.all_to_all(value_in, "seq", split_axis=0, concat_axis=1, tiled=True),
        lax.all_to_all(gate_inner, "seq", split_axis=0, concat_axis=1, tiled=True),
        lax.all_to_all(gate_outer, "seq", split_axis=0, concat_axis=1, tiled=True),
        lax.all_to_all(out_grad, "seq", split_axis=0, concat_axis=1, tiled=True),
    )
    count = value_cols.shape[0]
    length = value_cols.shape[1]
    first_row = seq_pos * count
    proj_rows = lax.dynamic_slice_in_dim(filter_proj, first_row, count, 1).astype(jnp.float32)
    rates = lax.dynamic_slice_in_dim(decay, first_row, count, 1)
    positions = lax.iota(jnp.float32, length)
    features = jnp.sin(frequency[None, :] * (positions[:, None] + 1.0))
    window = jnp.sqrt(2.0 * rates)[:, :, None] * jnp.exp(-rates[:, :, None] * positions)
    filters = jnp.einsum("kcf,tf->kct", proj_rows, features, precision=highest) * window
    value_f = value_cols.astype(jnp.float32)
    inner_f = inner_cols.astype(jnp.float32)
    spectra = forward_dft(jnp.concatenate([filters[0], filters[1], value_f], 0))
    inner_spec = rows_of(spectra, 0, count)
    outer_spec = rows_of(spectra, count, count)
    value_spec = rows_of(spectra, 2 * count, count)
    inner_act = inverse_dft(product_of(inner_spec, value_spec, False))
    mixed = inner_f * inner_act
    mixed_spec = forward_dft(mixed)
    outer_act = inverse_dft(product_of(outer_spec, mixed_spec, False))
    outer_f = outer_cols.astype(jnp.float32)
    grad_f = grad_cols.astype(jnp.float32)
    grad_outer = grad_f * outer_act
    grad_spec = forward_dft(grad_f * outer_f)
    outer_back = inverse_dft(
        joined(product_of(outer_spec, grad_spec, True), product_of(mixed_spec, grad_spec, True))
    )
    grad_mixed = outer_back[:count]
    grad_outer_filter = outer_back[count:]
    grad_inner = grad_mixed * inner_act
    inner_grad_spec = forward_dft(grad_mixed * inner_f)
    inner_back = inverse_dft(
        joined(
            product_of(inner_spec, inner_grad_spec, True),
            product_of(value_spec, inner_grad_spec, True),
        )
    )
    grad_value = inner_back[:count]
    grad_inner_filter = inner_back[count:]
    value_out, inner_out, outer_out = (
        lax.all_to_all(
            grad_value.astype(jnp.bfloat16), "seq", split_axis=1, concat_axis=0, tiled=True
        ),
        lax.all_to_all(
            grad_inner.astype(jnp.bfloat16), "seq", split_axis=1, concat_axis=0, tiled=True
        ),
        lax.all_to_all(
            grad_outer.astype(jnp.bfloat16), "seq", split_axis=1, concat_axis=0, tiled=True
        ),
    )
    weighted = jnp.stack([grad_inner_filter, grad_outer_filter]) * window
    own_grad = jnp.einsum("kct,tf->kcf", weighted, features, precision=highest)
    proj_grad = lax.all_gather(own_grad, "seq", axis=1, tiled=True)
    square_sum = lax.psum(jnp.sum(proj_grad * proj_grad), "ch")
    entries = proj_grad.size * lax.axis_size("ch")
    scale = lax.rsqrt(square_sum / entries + 1e-06)
    return (value_out, inner_out, outer_out, proj_grad * scale)


def body(value_in, gate_inner, gate_outer, out_grad, filter_proj, decay, frequency):
    seq_pos = lax.axis_index("seq")
    channels, lanes = value_in.shape
    count = channels // BLOCKS
    length = BLOCKS * lanes
    angle = jnp.asarray(angles())

    def own_rows(x):
        rows = lax.dynamic_slice_in_dim(x, seq_pos * count, count, 1)
        return rows.reshape((2 * count,) + x.shape[2:])

    received = exchanged(packed(value_in, gate_inner, gate_outer, out_grad), FIRST_PEERS)
    rates = own_rows(decay)
    features = jnp.sin(frequency[None, :] * (lax.iota(jnp.float32, length)[:, None] + 1.0))
    terms = jnp.concatenate(split_features(features), 1)
    spectra = filter_spectra(own_rows(filter_proj), rates, terms, angle)
    back = exchanged(operator_grads(received, rates, spectra, angle, terms), LAST_PEERS)
    at = {peer: i + 1 for i, peer in enumerate(LAST_PEERS)}
    near = [0] + [at[peer] for peer in LAST_PEERS if direct(peer)]
    held = near + [at[peer] for peer in HELD_FOR]
    for i, block in zip(held, lax.optimization_barrier([back[i] for i in held])):
        back[i] = block
    blocks = [back[i] for i in near]
    relayed = second_hop(blocks)
    own_sum = square_total(blocks, relayed)
    groups = lax.axis_size("ch")
    sums = [own_sum] + [
        lax.ppermute(own_sum, "ch", [(i, i ^ hop) for i in range(groups)]) for hop in range(1, groups)
    ]
    grads = unpacked(back, out_grad)
    proj_grad = scaled(blocks, relayed, sums, filter_proj.size * groups, features.shape[1])
    return (*grads, proj_grad.transpose(0, 2, 1))


def solution(mesh):
    def chosen(*arrays):
        whole = arrays[0].shape[1] == LANES and arrays[0].shape[0] % (BLOCKS * STEP) == 0
        fits = lax.axis_size("seq") == BLOCKS and lax.axis_size("ch") == 4
        return body(*arrays) if whole and fits else general_body(*arrays)

    split = P("ch", "seq")
    rows = P(None, "ch", None)
    return jax.shard_map(
        chosen,
        mesh=mesh,
        in_specs=(split, split, split, split, rows, P(None, "ch"), P()),
        out_specs=(split, split, split, rows),
        check_vma=False,
    )
```

```python
import math
import functools
import numpy as np
import ml_dtypes
import jax
import jax.numpy as jnp
from jax import lax
from jax.experimental import pallas as pl
from jax.experimental.pallas import tpu as pltpu
from jax.sharding import PartitionSpec as P

BLOCKS = 8
LANES = 128
COS1, COS2, COS3 = (math.cos(math.pi / 8), math.cos(math.pi / 4), math.cos(3 * math.pi / 8))
STEP = 16
HALVES = 1
SIN_AT, SIGN_AT = 16, 32
FIRST_PEERS = (1, 4, 2, 6, 3, 5, 7)
LAST_PEERS = (1, 4, 6, 2, 5, 7, 3)
HELD_FOR = (1,)
NEAR = 1
SENT, RETURNED = 3, 4
PACK_LIMIT, MAIN_LIMIT = 60, 32
PRODUCT_SCALE, OUTER_SCALE = 2.0**24, 2.0**-3


def angles():
    lane = np.arange(LANES)
    whole = 2 * np.pi * np.outer(lane, lane) / LANES
    turn = 2 * np.pi * np.outer(lane, np.arange(BLOCKS + 1)) / (2 * BLOCKS * LANES)
    turn[:, BLOCKS] += np.pi * lane
    columns = np.zeros((LANES, LANES))
    columns[:, : BLOCKS + 1] = np.cos(turn)
    columns[:, SIN_AT : SIN_AT + BLOCKS + 1] = np.sin(turn)
    columns[:, SIGN_AT] = 1.0 - 2.0 * (lane % 2)
    return np.stack([np.cos(whole), np.sin(whole), columns]).astype(np.float32)


def fold(x):
    s = [x[a] + x[a + 4] for a in range(4)]
    d = [x[a] - x[a + 4] for a in range(4)]
    t0, t1 = s[0] + s[2], s[1] + s[3]
    u0, u1 = s[0] - s[2], s[1] - s[3]
    p, w = (d[1] - d[3]) * COS2, (d[1] + d[3]) * COS2
    p1, p2, p3 = x[1] - x[7], (x[2] - x[6]) * COS2, x[3] - x[5]
    n1, n2, n3 = x[1] + x[7], (x[2] + x[6]) * COS2, x[3] + x[5]
    a0, b0 = x[0] + p2, x[0] - p2
    c0, d0 = p1 * COS1 + p3 * COS3, p1 * COS3 - p3 * COS1
    a1, b1 = n2 + x[4], n2 - x[4]
    c1, d1 = n1 * COS3 + n3 * COS1, n1 * COS1 - n3 * COS3
    return (
        (t0 + t1, t0 - t1),
        (a0 + c0, c1 + a1),
        (d[0] + p, d[2] + w),
        (b0 + d0, d1 + b1),
        (u0, u1),
        (b0 - d0, d1 - b1),
        (d[0] - p, w - d[2]),
        (a0 - c0, c1 - a1),
    )


def unfold(z):
    (z0, z8), (r1, i1), (r2, i2), (r3, i3), (r4, i4), (r5, i5), (r6, i6), (r7, i7) = z
    even, odd = z0 + z8, z0 - z8
    g = [even + r4, odd + i4, even - r4, odd - i4]
    dr, di = r2 - r6, i2 + i6
    h = [r2 + r6, (dr + di) * COS2, i2 - i6, (di - dr) * COS2]
    rs, rd, ts, td = r1 + r7, r1 - r7, r3 + r5, r3 - r5
    js, jd, ks, kd = i1 + i7, i1 - i7, i3 + i5, i3 - i5
    k = [None, rd * COS1 + td * COS3, (rs - ts) * COS2, rd * COS3 - td * COS1]
    m = [None, js * COS3 + ks * COS1, (jd + kd) * COS2, js * COS1 - ks * COS3]
    o = [rs + ts, k[1] + m[1], k[2] + m[2], k[3] + m[3], jd - kd, m[3] - k[3], m[2] - k[2], m[1] - k[1]]
    return [g[a] + h[a] + o[a] for a in range(4)] + [g[a] - h[a] + o[a + 4] for a in range(4)]


def fourth_power(x, scale):
    x = x * scale
    return (x * x * (x * jnp.abs(x))).astype(jnp.bfloat16)


def fourth_root(code, scale):
    code = code.astype(jnp.float32)
    size = jnp.sqrt(jnp.sqrt(jnp.abs(code))) * (1.0 / scale)
    return jnp.where(code < 0, -size, size)


def halves(x):
    high = x.astype(jnp.bfloat16)
    return high, (x - high.astype(jnp.float32)).astype(jnp.bfloat16)


def split_features(features):
    high = lax.reduce_precision(features, 8, 7)
    return high.astype(jnp.bfloat16), (features - high).astype(jnp.bfloat16)


def put(hi_ref, lo_ref, index, parts):
    for part, x in enumerate(parts):
        high, low = halves(x)
        lanes = slice(part * LANES, (part + 1) * LANES)
        hi_ref[index + (lanes,)] = high
        lo_ref[index + (lanes,)] = low


def store_folded(hi_ref, lo_ref, rows, blocks):
    for residue, parts in enumerate(fold(blocks)):
        put(hi_ref, lo_ref, (residue, rows), parts)


def make_table(angle, residue, table_hi, table_lo):
    def turned(column):
        cos, sin = angle[0], angle[1]
        turn_cos, turn_sin = angle[2, :, column : column + 1], angle[2, :, SIN_AT + column : SIN_AT + column + 1]
        return cos * turn_cos - sin * turn_sin, -(sin * turn_cos + cos * turn_sin)

    real, imag = turned(residue)
    if residue:
        blocks = ((real, imag), (imag, -real))
    else:
        lane = lax.broadcasted_iota(jnp.int32, real.shape, 1)
        below = lane < LANES // 2
        sign = jnp.broadcast_to(angle[2, :, SIGN_AT : SIGN_AT + 1], real.shape)
        top = jnp.where(below, real, 0.0), jnp.where(lane == 0, sign, jnp.where(below, imag, 0.0))
        blocks = (top, tuple(jnp.where(below, 0.0, x) for x in turned(BLOCKS)))
    for i, row in enumerate(blocks):
        for j, x in enumerate(row):
            high, low = halves(x)
            at = residue, slice(i * LANES, (i + 1) * LANES), slice(j * LANES, (j + 1) * LANES)
            table_hi[at] = high
            table_lo[at] = low


def times_transposed(high, low, table_hi, table_lo):
    def dot(x, table):
        return lax.dot_general(x, table, (((1,), (1,)), ((), ())), preferred_element_type=jnp.float32)

    return dot(high, table_hi) + (dot(low, table_hi) + dot(high, table_lo))


def times(high, low, table_hi, table_lo):
    dot = functools.partial(jnp.dot, preferred_element_type=jnp.float32)
    return dot(high, table_hi) + (dot(low, table_hi) + dot(high, table_lo))


def multiplied(left, right, conj, residue):
    a_re, a_im = left
    b_re, b_im = right
    rr, ii, ri, ir = a_re * b_re, a_im * b_im, a_re * b_im, a_im * b_re
    if conj:
        re, im = rr + ii, ri - ir
    else:
        re, im = rr - ii, ri + ir
    if residue == 0:
        shared = lax.broadcasted_iota(jnp.int32, re.shape, 1) == 0
        re, im = jnp.where(shared, 0.5 * rr, re), jnp.where(shared, 0.5 * ii, im)
    return re, im


def window_blocks(rate):
    rate = jnp.broadcast_to(rate, (rate.shape[0], LANES))
    place = lax.broadcasted_iota(jnp.int32, rate.shape, 1).astype(jnp.float32)
    first = jnp.sqrt(2.0 * rate) * jnp.exp(-rate * place) * (1.0 / (BLOCKS * LANES))
    return [first * jnp.exp(rate * (-float(LANES) * a)) if a else first for a in range(BLOCKS)]


def fetched(sources, places, sems):
    copies = [pltpu.make_async_copy(src, dst, sems.at[i]) for i, (src, dst) in enumerate(zip(sources, places))]
    for copy in copies:
        copy.start()
    return copies


def filter_kernel(proj, rate, features, angle, spectra, filters, fold_hi, fold_lo, table_hi, table_lo):
    rows = proj.shape[0]
    for a in range(BLOCKS):
        terms = features[a * LANES : (a + 1) * LANES]
        filters[a] = lax.dot_general(proj[...], terms, (((1,), (1,)), ((), ())), preferred_element_type=jnp.float32)

    @pl.loop(0, rows // STEP)
    def _(step):
        at = pl.ds(pl.multiple_of(step * STEP, STEP), STEP)
        window = window_blocks(rate[at, :])
        store_folded(fold_hi, fold_lo, at, [filters[a, at, :] * window[a] for a in range(BLOCKS)])

    for residue in range(BLOCKS):
        make_table(angle, residue, table_hi, table_lo)
        spectra[residue] = times(fold_hi[residue], fold_lo[residue], table_hi[residue], table_lo[residue])


def direct(peer):
    return not peer & NEAR


def places(peers):
    place = lax.axis_index("seq")
    return [place] + [place ^ peer for peer in peers]


def interleaved(*lists):
    steps = [((i + 0.5) / len(steps), n, step) for n, steps in enumerate(lists) for i, step in enumerate(steps)]
    for _, _, step in sorted(steps, key=lambda entry: entry[:2]):
        step()


def main_kernel(*refs):
    received, (rate, filt, angle, features), sent = refs[:BLOCKS], refs[BLOCKS : BLOCKS + 4], refs[BLOCKS + 4 : 2 * BLOCKS + 4]
    (
        moved, results, one_hi, one_lo, two_hi, two_lo, spec, back, weighted_hi, weighted_lo, total, table_hi, table_lo,
    ) = refs[2 * BLOCKS + 4 :]
    count = moved.shape[1] // SENT
    part = count // HALVES
    value, inner, product = (moved.at[:, i * count : (i + 1) * count] for i in range(SENT))
    grad_value, grad_inner, outer_coded = (results.at[:, i * count : (i + 1) * count] for i in range(3))
    for place, block in zip(places(FIRST_PEERS), received):
        moved[place] = block[...]
    dot = functools.partial(jnp.dot, preferred_element_type=jnp.float32)
    upper, lower = slice(0, part), slice(part, 2 * part)

    def forward(half, residue):
        return times(one_hi[residue, half], one_lo[residue, half], table_hi[residue], table_lo[residue])

    def inverse(half, residue, rows):
        back[residue, half, rows] = times_transposed(
            two_hi[residue, half, rows], two_lo[residue, half, rows], table_hi[residue], table_lo[residue])

    def pair(ref, residue, half, rows):
        return ref[residue, half, rows, :LANES], ref[residue, half, rows, LANES:]

    def filter_pair(residue, half, place):
        rows = slice(place * count + half * part, place * count + (half + 1) * part)
        return filt[residue, rows, :LANES], filt[residue, rows, LANES:]

    def rows_of(half, step):
        first = half * part + step * STEP
        return slice(first, first + STEP), slice(step * STEP, (step + 1) * STEP)

    def signal(half, place, step):
        first = place * part + step * STEP
        return unfold([pair(back, residue, half, slice(first, first + STEP)) for residue in range(BLOCKS)])

    def fold_inputs(half, step, place):
        at, _ = rows_of(half, step)
        first = place * part + step * STEP
        if place == 0:
            blocks = [value[a, at, :].astype(jnp.float32) for a in range(BLOCKS)]
        else:
            blocks = [fourth_root(product[a, at, :], PRODUCT_SCALE) for a in range(BLOCKS)]
        store_folded(one_hi.at[:, half], one_lo.at[:, half], slice(first, first + STEP), blocks)

    def first_class(half, residue):
        if half == 0:
            make_table(angle, residue, table_hi, table_lo)
        spec[residue, half] = forward(half, residue)
        for place, rows in ((0, upper), (1, lower)):
            put(two_hi, two_lo, (residue, half, rows), multiplied(
                filter_pair(residue, half, place), pair(spec, residue, half, rows), place == 1, residue))
        inverse(half, residue, slice(0, 2 * part))

    def between(half, step):
        at, first = rows_of(half, step)
        second = slice(part + first.start, part + first.stop)
        gate = [inner[a, at, :].astype(jnp.float32) for a in range(BLOCKS)]
        inner_act = signal(half, 0, step)
        store_folded(one_hi.at[:, half], one_lo.at[:, half], first, [gate[a] * inner_act[a] for a in range(BLOCKS)])
        grad_mixed = signal(half, 1, step)
        for a in range(BLOCKS):
            grad_inner[a, at, :] = (grad_mixed[a] * inner_act[a]).astype(jnp.bfloat16)
        store_folded(one_hi.at[:, half], one_lo.at[:, half], second, [gate[a] * grad_mixed[a] for a in range(BLOCKS)])

    def second_class(half, residue):
        both = forward(half, residue)
        mixed = both[upper, :LANES], both[upper, LANES:]
        inner_grad = both[lower, :LANES], both[lower, LANES:]
        products = (
            multiplied(filter_pair(residue, half, 1), mixed, False, residue),
            multiplied(filter_pair(residue, half, 0), inner_grad, True, residue),
            multiplied(pair(spec, residue, half, upper), inner_grad, True, residue),
            multiplied(mixed, pair(spec, residue, half, lower), True, residue),
        )
        for place, product in enumerate(products):
            put(two_hi, two_lo, (residue, half, slice(place * part, (place + 1) * part)), product)
        inverse(half, residue, slice(2 * part, 4 * part))

    def third_class(half, residue):
        inverse(half, residue, slice(0, 2 * part))

    def outputs(half, step, place):
        at, rows = rows_of(half, step)
        blocks = signal(half, place, step)
        if place == 0:
            for a in range(BLOCKS):
                outer_coded[a, at, :] = fourth_power(blocks[a], OUTER_SCALE)
        elif place == 1:
            for a in range(BLOCKS):
                grad_value[a, at, :] = blocks[a].astype(jnp.bfloat16)
        else:
            which = place - 2
            window = window_blocks(rate[which * count + at.start : which * count + at.stop, :])
            rows = slice(which * part + rows.start, which * part + rows.stop)
            for a in range(BLOCKS):
                high, low = halves(blocks[a] * window[a])
                lanes = slice(a * LANES, (a + 1) * LANES)
                weighted_hi[half, rows, lanes] = high
                weighted_lo[half, rows, lanes] = low

    def project(half):
        both = dot(weighted_hi[half], features[...]) + dot(weighted_lo[half], features[...])
        for which in range(2):
            first = which * count + half * part
            total[first : first + part] = both[which * part : (which + 1) * part]

    def steps(function, half, *others):
        calls = BLOCKS if function in (first_class, second_class, third_class) else part // STEP
        return [
            functools.partial(function, half, i, *other) for i in range(calls) for other in (others or ((),))
        ]

    for half in range(HALVES):
        interleaved(steps(fold_inputs, half, (0,), (1,)))
        interleaved(steps(first_class, half))
        interleaved(steps(between, half))
        interleaved(steps(second_class, half))
        interleaved(steps(third_class, half), steps(outputs, half, (2,), (3,)))
        project(half)
        interleaved(steps(outputs, half, (0,), (1,)))

    whole = total[...].T
    width = whole.shape[0] // 2
    whole = whole[:width] + whole[width:]
    for place in range(2):
        piece = whole[:, place * count : (place + 1) * count]
        coded = (piece * jnp.abs(piece)).astype(jnp.bfloat16)
        for a in range(BLOCKS):
            results[a, 3 * count + place * width : 3 * count + (place + 1) * width] = coded
    for place, block in zip(places(LAST_PEERS), sent):
        block[...] = results[place, : block.shape[0]]


def device_call(kernel, out_shape, scratch, in_vmem, out_vmem, name, limit):
    def spec(inside):
        return pl.BlockSpec(memory_space=pltpu.VMEM if inside else pl.ANY)

    return pl.pallas_call(
        kernel,
        out_shape=out_shape,
        in_specs=[spec(inside) for inside in in_vmem],
        out_specs=[spec(inside) for inside in out_vmem],
        scratch_shapes=scratch,
        compiler_params=pltpu.CompilerParams(vmem_limit_bytes=limit * 2**20),
        name=name,
    )


def filter_spectra(proj_rows, rates, terms, angle):
    rows = proj_rows.shape[0]
    twice = jnp.concatenate([proj_rows, proj_rows], 1)
    bf, f32 = jnp.bfloat16, jnp.float32
    width = 2 * LANES
    return device_call(
        filter_kernel,
        [jax.ShapeDtypeStruct((BLOCKS, rows, width), f32)],
        [pltpu.VMEM((BLOCKS, rows, LANES), f32)]
        + [pltpu.VMEM((BLOCKS, rows, width), bf)] * 2
        + [pltpu.VMEM((BLOCKS, width, width), bf)] * 2,
        (True,) * 4,
        (True,),
        "filter_spectra",
        16,
    )(twice, rates.reshape(rows, 1), terms, angle)[0]


def operator_grads(received, rates, spectra, angle, terms):
    count = received[0].shape[0] // SENT
    part = count // HALVES
    bf, f32 = jnp.bfloat16, jnp.float32
    width = 2 * LANES
    return device_call(
        main_kernel,
        [jax.ShapeDtypeStruct(((3 + direct(peer)) * count, LANES), bf) for peer in (0,) + LAST_PEERS],
        [pltpu.VMEM((BLOCKS, SENT * count, LANES), bf), pltpu.VMEM((BLOCKS, RETURNED * count, LANES), bf)]
        + [pltpu.VMEM((BLOCKS, HALVES, 2 * part, width), bf)] * 2
        + [pltpu.VMEM((BLOCKS, HALVES, 4 * part, width), bf)] * 2
        + [pltpu.VMEM((BLOCKS, HALVES, 2 * part, width), f32), pltpu.VMEM((BLOCKS, HALVES, 4 * part, width), f32)]
        + [pltpu.VMEM((HALVES, 2 * part, BLOCKS * LANES), bf)] * 2
        + [pltpu.VMEM((2 * count, LANES), f32)]
        + [pltpu.VMEM((BLOCKS, width, width), bf)] * 2,
        (True,) * (BLOCKS + 4),
        (True,) * BLOCKS,
        "operator_grads",
        MAIN_LIMIT,
    )(*received, rates.reshape(2 * count, 1), spectra, angle, terms)


def pack_kernel(value, inner, outer, grad, *refs):
    sent, (outer_in, grad_in, sems) = refs[:BLOCKS], refs[BLOCKS:]
    count = sent[0].shape[0] // SENT
    first = fetched((outer, grad), (outer_in, grad_in), sems)
    rest = []
    for i, (place, block) in enumerate(zip(places(FIRST_PEERS), sent)):
        for j, source in enumerate((value, inner)):
            copy = pltpu.make_async_copy(source.at[place], block.at[j * count : (j + 1) * count], sems.at[2 + 2 * i + j])
            copy.start()
            rest.append(copy)
    for copy in first:
        copy.wait()
    for place, block in zip(places(FIRST_PEERS), sent):
        both = grad_in[place].astype(jnp.float32) * outer_in[place].astype(jnp.float32)
        block[2 * count :] = fourth_power(both, PRODUCT_SCALE)
    for copy in rest:
        copy.wait()


def packed(*arrays):
    channels, lanes = arrays[0].shape
    count = channels // BLOCKS
    held = pltpu.VMEM((BLOCKS, count, lanes), jnp.bfloat16)
    return device_call(
        pack_kernel,
        [jax.ShapeDtypeStruct((SENT * count, lanes), jnp.bfloat16)] * BLOCKS,
        [held, held, pltpu.SemaphoreType.DMA((2 + 2 * BLOCKS,))],
        (False,) * 4,
        (True,) * BLOCKS,
        "packed",
        PACK_LIMIT,
    )(*(x.reshape(BLOCKS, count, lanes) for x in arrays))


def exchanged(blocks, peers):
    swaps = [[(i, i ^ peer) for i in range(BLOCKS)] for peer in peers]
    return [blocks[0]] + [lax.ppermute(block, "seq", swap) for block, swap in zip(blocks[1:], swaps)]


def gather_kernel(*refs):
    received, out = refs[:-1], refs[-1]
    count = out.shape[0] // len(received)
    for i, block in enumerate(received):
        out[i * count : (i + 1) * count] = block[3 * count :]


def second_hop(blocks):
    count = blocks[0].shape[0] // RETURNED
    gathered = device_call(
        gather_kernel,
        [jax.ShapeDtypeStruct((len(blocks) * count, LANES), jnp.bfloat16)],
        [],
        (True,) * len(blocks),
        (True,),
        "gather_proj",
        16,
    )(*blocks)[0]
    return lax.ppermute(gathered, "seq", [(i, i ^ NEAR) for i in range(BLOCKS)])


def proj_parts(direct_blocks, relayed):
    peers = [0] + [peer for peer in LAST_PEERS if direct(peer)]
    count = relayed.shape[0] // len(peers)
    for peer, block in zip(peers, direct_blocks):
        yield peer, block[3 * count :].astype(jnp.float32)
    for i, peer in enumerate(peers):
        yield peer ^ NEAR, relayed[i * count : (i + 1) * count].astype(jnp.float32)


def sum_kernel(*refs):
    *blocks, relayed, total = refs
    part = jnp.zeros(total.shape, jnp.float32)
    for _, coded in proj_parts(blocks, relayed):
        part = part + jnp.sum(jnp.abs(coded).reshape((-1,) + total.shape), 0)
    total[...] = jnp.broadcast_to(jnp.sum(part, keepdims=True), total.shape)


def square_total(blocks, relayed):
    return device_call(
        sum_kernel,
        [jax.ShapeDtypeStruct((8, LANES), jnp.float32)],
        [],
        (True,) * (len(blocks) + 1),
        (True,),
        "square_total",
        16,
    )(*blocks, relayed)[0]


def unpack_kernel(*refs):
    received, (grad, *outs), (grad_in, outer_out, sems) = refs[:BLOCKS], refs[BLOCKS : BLOCKS + 4], refs[BLOCKS + 4 :]
    count = grad.shape[1]
    fetch = pltpu.make_async_copy(grad, grad_in, sems.at[2 * BLOCKS])
    fetch.start()
    copies = []
    for i, (place, block) in enumerate(zip(places(LAST_PEERS), received)):
        for j, out in enumerate(outs[:2]):
            copy = pltpu.make_async_copy(block.at[j * count : (j + 1) * count], out.at[place], sems.at[2 * i + j])
            copy.start()
            copies.append(copy)
    fetch.wait()
    for place, block in zip(places(LAST_PEERS), received):
        act = fourth_root(block[2 * count : 3 * count], OUTER_SCALE)
        outer_out[place] = (grad_in[place].astype(jnp.float32) * act).astype(jnp.bfloat16)
    last = pltpu.make_async_copy(outer_out, outs[2], sems.at[2 * BLOCKS + 1])
    last.start()
    for copy in (*copies, last):
        copy.wait()


def unpacked(received, grad):
    channels, lanes = grad.shape
    count = channels // BLOCKS
    block = jax.ShapeDtypeStruct((BLOCKS, count, lanes), jnp.bfloat16)
    held = pltpu.VMEM(block.shape, block.dtype)
    grads = device_call(
        unpack_kernel,
        [block] * 3,
        [held, held, pltpu.SemaphoreType.DMA((2 * BLOCKS + 2,))],
        (True,) * BLOCKS + (False,),
        (False,) * 3,
        "unpacked",
        16,
    )(*received, grad.reshape(block.shape))
    return [x.reshape(channels, lanes) for x in grads]


def scale_kernel(entries, blocks, *refs):
    received, relayed, sums, (out, held, sem) = refs[:blocks], refs[blocks], refs[blocks + 1 : -3], refs[-3:]
    total = sums[0][...]
    for part in sums[1:]:
        total = total + part[...]
    scale = lax.rsqrt(total * (1.0 / entries) + 1e-06)[:1]
    features = held.shape[1]
    own = lax.axis_index("seq")
    for peer, coded in proj_parts(received, relayed):
        lanes = pl.ds(pl.multiple_of((own ^ peer) * LANES, LANES), LANES)
        size = jnp.sqrt(jnp.abs(coded)) * scale
        both = jnp.where(coded < 0, -size, size)
        for i in range(2):
            held[i, :, lanes] = both[i * features : (i + 1) * features]
    copy = pltpu.make_async_copy(held, out, sem)
    copy.start()
    copy.wait()


def scaled(blocks, relayed, sums, entries, features):
    shape = (2, features, BLOCKS * LANES)
    return device_call(
        functools.partial(scale_kernel, entries, len(blocks)),
        [jax.ShapeDtypeStruct(shape, jnp.float32)],
        [pltpu.VMEM(shape, jnp.float32), pltpu.SemaphoreType.DMA],
        (True,) * (len(blocks) + 1 + len(sums)),
        (False,),
        "scaled",
        16,
    )(*blocks, relayed, *sums)[0]


highest = lax.Precision.HIGHEST


def angle_table(rows, cols, period):
    row_idx = lax.broadcasted_iota(jnp.int32, (rows, cols), 0)
    col_idx = lax.broadcasted_iota(jnp.int32, (rows, cols), 1)
    angle = (row_idx * col_idx % period).astype(jnp.float32) * (2.0 * math.pi / period)
    return (jnp.cos(angle), jnp.sin(angle))


def split_length(total):
    return max((factor for factor in range(2, math.isqrt(total) + 1, 2) if total % factor == 0))


def forward_dft(signal):
    rows, length = signal.shape
    total = 2 * length
    first = split_length(total)
    second = total // first
    half = first // 2
    shaped = signal.reshape(rows, half, second)
    cos_one, sin_one = angle_table(half, first, first)
    part_re = jnp.einsum("mab,ak->mkb", shaped, cos_one, precision=highest)
    part_im = -jnp.einsum("mab,ak->mkb", shaped, sin_one, precision=highest)
    twist_cos, twist_sin = angle_table(first, second, total)
    turned_re = part_re * twist_cos + part_im * twist_sin
    turned_im = part_im * twist_cos - part_re * twist_sin
    cos_two, sin_two = angle_table(second, second, second)
    out_re = jnp.einsum("mkb,bl->mkl", turned_re, cos_two, precision=highest) + jnp.einsum(
        "mkb,bl->mkl", turned_im, sin_two, precision=highest
    )
    out_im = jnp.einsum("mkb,bl->mkl", turned_im, cos_two, precision=highest) - jnp.einsum(
        "mkb,bl->mkl", turned_re, sin_two, precision=highest
    )
    return (out_re, out_im)


def inverse_dft(spectrum):
    spec_re, spec_im = spectrum
    rows, first, second = spec_re.shape
    total = first * second
    half = first // 2
    cos_two, sin_two = angle_table(second, second, second)
    part_re = jnp.einsum("mkl,lb->mkb", spec_re, cos_two, precision=highest) - jnp.einsum(
        "mkl,lb->mkb", spec_im, sin_two, precision=highest
    )
    part_im = jnp.einsum("mkl,lb->mkb", spec_re, sin_two, precision=highest) + jnp.einsum(
        "mkl,lb->mkb", spec_im, cos_two, precision=highest
    )
    twist_cos, twist_sin = angle_table(first, second, total)
    turned_re = part_re * twist_cos - part_im * twist_sin
    turned_im = part_re * twist_sin + part_im * twist_cos
    cos_one, sin_one = angle_table(half, first, first)
    result = jnp.einsum("mkb,ak->mab", turned_re, cos_one, precision=highest) - jnp.einsum(
        "mkb,ak->mab", turned_im, sin_one, precision=highest
    )
    return result.reshape(rows, half * second) / total


def product_of(left, right, conj_left):
    left_re, left_im = left
    right_re, right_im = right
    if conj_left:
        left_im = -left_im
    return (left_re * right_re - left_im * right_im, left_re * right_im + left_im * right_re)


def rows_of(spectrum, start, count):
    return (spectrum[0][start : start + count], spectrum[1][start : start + count])


def joined(upper, lower):
    return (jnp.concatenate([upper[0], lower[0]], 0), jnp.concatenate([upper[1], lower[1]], 0))


def general_body(value_in, gate_inner, gate_outer, out_grad, filter_proj, decay, frequency):
    seq_pos = lax.axis_index("seq")
    value_cols, inner_cols, outer_cols, grad_cols = (
        lax.all_to_all(value_in, "seq", split_axis=0, concat_axis=1, tiled=True),
        lax.all_to_all(gate_inner, "seq", split_axis=0, concat_axis=1, tiled=True),
        lax.all_to_all(gate_outer, "seq", split_axis=0, concat_axis=1, tiled=True),
        lax.all_to_all(out_grad, "seq", split_axis=0, concat_axis=1, tiled=True),
    )
    count = value_cols.shape[0]
    length = value_cols.shape[1]
    first_row = seq_pos * count
    proj_rows = lax.dynamic_slice_in_dim(filter_proj, first_row, count, 1).astype(jnp.float32)
    rates = lax.dynamic_slice_in_dim(decay, first_row, count, 1)
    positions = lax.iota(jnp.float32, length)
    features = jnp.sin(frequency[None, :] * (positions[:, None] + 1.0))
    window = jnp.sqrt(2.0 * rates)[:, :, None] * jnp.exp(-rates[:, :, None] * positions)
    filters = jnp.einsum("kcf,tf->kct", proj_rows, features, precision=highest) * window
    value_f = value_cols.astype(jnp.float32)
    inner_f = inner_cols.astype(jnp.float32)
    spectra = forward_dft(jnp.concatenate([filters[0], filters[1], value_f], 0))
    inner_spec = rows_of(spectra, 0, count)
    outer_spec = rows_of(spectra, count, count)
    value_spec = rows_of(spectra, 2 * count, count)
    inner_act = inverse_dft(product_of(inner_spec, value_spec, False))
    mixed = inner_f * inner_act
    mixed_spec = forward_dft(mixed)
    outer_act = inverse_dft(product_of(outer_spec, mixed_spec, False))
    outer_f = outer_cols.astype(jnp.float32)
    grad_f = grad_cols.astype(jnp.float32)
    grad_outer = grad_f * outer_act
    grad_spec = forward_dft(grad_f * outer_f)
    outer_back = inverse_dft(
        joined(product_of(outer_spec, grad_spec, True), product_of(mixed_spec, grad_spec, True))
    )
    grad_mixed = outer_back[:count]
    grad_outer_filter = outer_back[count:]
    grad_inner = grad_mixed * inner_act
    inner_grad_spec = forward_dft(grad_mixed * inner_f)
    inner_back = inverse_dft(
        joined(
            product_of(inner_spec, inner_grad_spec, True),
            product_of(value_spec, inner_grad_spec, True),
        )
    )
    grad_value = inner_back[:count]
    grad_inner_filter = inner_back[count:]
    value_out, inner_out, outer_out = (
        lax.all_to_all(
            grad_value.astype(jnp.bfloat16), "seq", split_axis=1, concat_axis=0, tiled=True
        ),
        lax.all_to_all(
            grad_inner.astype(jnp.bfloat16), "seq", split_axis=1, concat_axis=0, tiled=True
        ),
        lax.all_to_all(
            grad_outer.astype(jnp.bfloat16), "seq", split_axis=1, concat_axis=0, tiled=True
        ),
    )
    weighted = jnp.stack([grad_inner_filter, grad_outer_filter]) * window
    own_grad = jnp.einsum("kct,tf->kcf", weighted, features, precision=highest)
    proj_grad = lax.all_gather(own_grad, "seq", axis=1, tiled=True)
    square_sum = lax.psum(jnp.sum(proj_grad * proj_grad), "ch")
    entries = proj_grad.size * lax.axis_size("ch")
    scale = lax.rsqrt(square_sum / entries + 1e-06)
    return (value_out, inner_out, outer_out, proj_grad * scale)


def body(value_in, gate_inner, gate_outer, out_grad, filter_proj, decay, frequency):
    seq_pos = lax.axis_index("seq")
    channels, lanes = value_in.shape
    count = channels // BLOCKS
    length = BLOCKS * lanes
    angle = jnp.asarray(angles())

    def own_rows(x):
        rows = lax.dynamic_slice_in_dim(x, seq_pos * count, count, 1)
        return rows.reshape((2 * count,) + x.shape[2:])

    received = exchanged(packed(value_in, gate_inner, gate_outer, out_grad), FIRST_PEERS)
    rates = own_rows(decay)
    features = jnp.sin(frequency[None, :] * (lax.iota(jnp.float32, length)[:, None] + 1.0))
    terms = jnp.concatenate(split_features(features), 1)
    spectra = filter_spectra(own_rows(filter_proj), rates, terms, angle)
    back = exchanged(operator_grads(received, rates, spectra, angle, terms), LAST_PEERS)
    at = {peer: i + 1 for i, peer in enumerate(LAST_PEERS)}
    near = [0] + [at[peer] for peer in LAST_PEERS if direct(peer)]
    held = near + [at[peer] for peer in HELD_FOR]
    for i, block in zip(held, lax.optimization_barrier([back[i] for i in held])):
        back[i] = block
    blocks = [back[i] for i in near]
    relayed = second_hop(blocks)
    own_sum = square_total(blocks, relayed)
    groups = lax.axis_size("ch")
    sums = [own_sum] + [
        lax.ppermute(own_sum, "ch", [(i, i ^ hop) for i in range(groups)]) for hop in range(1, groups)
    ]
    grads = unpacked(back, out_grad)
    proj_grad = scaled(blocks, relayed, sums, filter_proj.size * groups, features.shape[1])
    return (*grads, proj_grad.transpose(0, 2, 1))


def solution(mesh):
    def chosen(*arrays):
        whole = arrays[0].shape[1] == LANES and arrays[0].shape[0] % (BLOCKS * STEP) == 0
        fits = lax.axis_size("seq") == BLOCKS and lax.axis_size("ch") == 4
        return body(*arrays) if whole and fits else general_body(*arrays)

    split = P("ch", "seq")
    rows = P(None, "ch", None)
    return jax.shard_map(
        chosen,
        mesh=mesh,
        in_specs=(split, split, split, split, rows, P(None, "ch"), P()),
        out_specs=(split, split, split, rows),
        check_vma=False,
    )
```
